256 devices in a mesh: dp: 32 (over x, y, core), vocab: 8 (over z).
Axes of the slice: x: 4, y: 4, z: 8, core: 2. Of those that a mesh axis runs over, the one named last changes fastest.
Arguments:
- queries: bfloat16 [1024, 4096], P('dp', 'vocab'), may hold values from -1200 to 1200
- own_keys: bfloat16 [1024, 2048], P('dp', 'vocab'), may hold values from -8 to 8
- own_values: bfloat16 [1024, 2048], P('dp', 'vocab'), may hold values from -6 to 6
- prompt_keys: bfloat16 [32, 128, 2048], P('dp', None, 'vocab'), may hold values from -6 to 6
- prompt_values: bfloat16 [32, 128, 2048], P('dp', None, 'vocab'), may hold values from -6 to 6
- prompt_lengths: int32 [32], replicated, may hold values from 1 to 128
- completion_prompt: int32 [128], replicated, may hold values from 0 to 31, as said below
- completion_lengths: int32 [128], replicated, may hold values from 2 to 8
- targets: int32 [1024], replicated, may hold values from 0 to 131071
- advantages: float32 [128], replicated, may hold values from -4 to 4
- residual: bfloat16 [1024, 5376], P('dp'), may hold values from -16 to 16
- out_proj: bfloat16 [4096, 5376], P('vocab'), may hold values from -0.25 to 0.25
- norm_gain: float32 [5376], replicated, may hold values from 0.5 to 1.5
- embedding: bfloat16 [131072, 5376], P(('dp', 'vocab')), may hold values from -4 to 4
Outputs:
- logprob: float32 [1024], P('dp')
- hidden_grad: float32 [1024, 5376], P('dp')
The draws below stay inside these ranges and needn't reach their ends.
Inputs may be any that keep to these rules, and one draw needn't show every extreme that they name: `completion_prompt`: each prompt is named by the same number of completions.
All inputs are finite; a program needn't handle non-finite values.
Results may differ from the reference program's by a relative error of at most 0.023.
Values may be sent and summed in bfloat16 or wider, within the bound.
No kernel may reach another device: no remote copies, remote signals or barrier semaphores. Data moves between devices by JAX's collectives and lax.ppermute only.
A program may use at most 128 MiB of HBM per device.

```python
import jax
import jax.numpy as jnp
from jax import lax

D = 5376
HEADS = 32
KVHEADS = 16
HDIM = 128
VDEV = 512
CLEN = 8
PLEN = 128
COMPS = 128
PROMPTS = 32
ROWS_ALL = 1024
VOCAB = 131072
N_DP = 32
N_VOCAB = 8


def grouped_rows(key, row_ids, group_ids):
    centre_key = jax.random.fold_in(key, 7)

    def one_row(row_id, group_id):
        centre = jax.random.normal(jax.random.fold_in(centre_key, group_id), (D,), jnp.float32)
        spread = jax.random.normal(jax.random.fold_in(key, row_id), (D,), jnp.float32)
        return 0.95 * centre + 0.3 * spread
    return jax.vmap(one_row)(row_ids, group_ids)


def shared_keys(key):
    return jax.random.normal(jax.random.fold_in(key, 9001), (COMPS * CLEN, KVHEADS * HDIM), jnp.float32)


def chosen_completions(key):
    chosen = jax.random.randint(jax.random.fold_in(key, 9002), (COMPS,), 0, 8) == 0
    levels = jnp.array([150.0, 220.0, 320.0], jnp.float32)
    level = levels[jax.random.randint(jax.random.fold_in(key, 9003), (COMPS,), 0, 3)]
    return (chosen, level)


def ragged(key, total_count, lowest, highest):
    drawn = jax.random.randint(jax.random.fold_in(key, 1), (total_count,), lowest, highest + 1)
    longest = jax.random.randint(jax.random.fold_in(key, 2), (), 0, total_count)
    offset = jax.random.randint(jax.random.fold_in(key, 3), (), 1, total_count)
    shortest = (longest + offset) % total_count
    return drawn.at[longest].set(highest).at[shortest].set(lowest).astype(jnp.int32)


def draw_queries(key, part):
    anchor = key
    key = jax.random.fold_in(key, 13)
    drawn = jax.random.normal(key, (COMPS * CLEN, HEADS * HDIM), jnp.float32)
    chosen, level = chosen_completions(anchor)
    strength = level * 168.0 ** 0.5 / HDIM
    leading = shared_keys(anchor).reshape(COMPS, CLEN, KVHEADS, HDIM)[:, 0]
    aligned = jnp.repeat(leading, HEADS // KVHEADS, axis=1).reshape(COMPS, HEADS * HDIM) * strength[:, None]
    grid = drawn.reshape(COMPS, CLEN, HEADS * HDIM)
    grid = grid.at[:, 1].set(jnp.where(chosen[:, None], aligned, grid[:, 1]))
    drawn = grid.reshape(COMPS * CLEN, HEADS * HDIM)
    return jnp.clip(drawn, -1200.0, 1200.0).astype(jnp.bfloat16)


def draw_own_keys(key, part):
    anchor = key
    key = jax.random.fold_in(key, 14)
    drawn = shared_keys(anchor)
    chosen, level = chosen_completions(anchor)
    closeness = 2.0 * HDIM ** 0.5 / level
    grid = drawn.reshape(COMPS, CLEN, KVHEADS * HDIM)
    nearby = grid[:, 0] + closeness[:, None] * jax.random.normal(key, (COMPS, KVHEADS * HDIM), jnp.float32)
    grid = grid.at[:, 1].set(jnp.where(chosen[:, None], nearby, grid[:, 1]))
    drawn = grid.reshape(COMPS * CLEN, KVHEADS * HDIM)
    return jnp.clip(drawn, -8.0, 8.0).astype(jnp.bfloat16)


def draw_residual(key, part):
    key = jax.random.fold_in(key, 12)
    drawn = 0.1 * jax.random.normal(jax.random.fold_in(key, 1), (COMPS * CLEN, D), jnp.float32)
    return jnp.clip(drawn, -16.0, 16.0).astype(jnp.bfloat16)


def draw_embedding(key, part):
    row_ids = jnp.arange(VOCAB, dtype=jnp.int32)
    key = jax.random.fold_in(key, 11)
    group_count = max(VOCAB // 1024, 2)
    group_ids = (jax.random.permutation(jax.random.fold_in(key, 3), VOCAB) % group_count).astype(jnp.int32)
    drawn = 3.3 * D ** (-0.5) * grouped_rows(key, row_ids, group_ids)
    return jnp.clip(drawn, -4.0, 4.0).astype(jnp.bfloat16)


def draw_completion_prompt(key, part):
    key = jax.random.fold_in(key, 15)
    shuffled = jax.random.permutation(key, COMPS)
    return (shuffled % PROMPTS).astype(jnp.int32)


def draw_completion_lengths(key, part):
    key = jax.random.fold_in(key, 16)
    return ragged(key, COMPS, 2, CLEN)


def draw_prompt_lengths(key, part):
    key = jax.random.fold_in(key, 17)
    return ragged(key, PROMPTS, 1, PLEN)


def plant(values, key, low, largest):
    longest = values.shape.index(max(values.shape))
    spots = []
    for shift in (0, 1):
        where = [jax.random.randint(jax.random.fold_in(key, axis), (), 0, length) for axis, length in enumerate(values.shape)]
        where[longest] = (where[longest] + shift) % values.shape[longest]
        spots.append(tuple(where))
    return values.at[spots[0]].set(low).at[spots[1]].set(largest)


def with_spikes(entries, rng, source, target, blocks, factor):
    owner, partner = [(jnp.arange(entries.shape[dim]) // (entries.shape[dim] // blocks)).reshape([-1 if axis == dim else 1 for axis in range(entries.ndim)]) for dim in (source, target)]
    chosen = jax.random.permutation(rng, blocks)[partner]
    strong = (owner == chosen) | (owner == (partner + blocks // 2) % blocks)
    return jnp.where(strong, factor * entries, entries)


def shard_levels(own_key, extent, pieces, least, top_value):
    factor_of, own = 1.0, jax.random.fold_in(own_key, 6)
    for dim, blocks in pieces:
        heights = jnp.exp(jax.random.uniform(jax.random.fold_in(own, dim), (blocks,), jnp.float32, least / len(pieces), top_value / len(pieces)))
        factor_of = factor_of * jnp.repeat(heights, extent[dim] // blocks).reshape([-1 if axis == dim else 1 for axis in range(len(extent))])
    return factor_of


def scatter_about(own_key, extent, deviation, bound, shards=(), kind=jnp.bfloat16):
    loudness = shard_levels(own_key, extent, shards, -0.22, 0.18) if shards else 1.0
    values = jax.random.normal(own_key, extent, jnp.float32) * deviation * loudness
    return jnp.minimum(jnp.maximum(values, -bound), bound).astype(kind)


def bell_draw_with(own_key, extent, deviation, reach, split, heavy, kind=jnp.bfloat16):
    result = deviation * jax.random.normal(own_key, extent, jnp.float32)
    if split:
        result = result * shard_levels(own_key, extent, split, -0.22, 0.18)
    return jnp.clip(with_spikes(result, jax.random.fold_in(own_key, 3), *heavy), -reach, reach).astype(kind)


def setup_inputs(seed: int = 0) -> dict:
    streams_of = jax.random.split(jax.random.key(seed), 15)
    queries = draw_queries(jax.random.fold_in(streams_of[14], 71), 0)
    own_keys = draw_own_keys(jax.random.fold_in(streams_of[14], 71), 0)
    own_values = scatter_about(streams_of[2], (ROWS_ALL, KVHEADS * HDIM), 1.0, 6.0, ((0, 32), (1, 8)))
    prompt_keys = scatter_about(streams_of[3], (PROMPTS, PLEN, KVHEADS * HDIM), 1.0, 6.0, ((0, 32), (2, 8)))
    prompt_values = scatter_about(streams_of[4], (PROMPTS, PLEN, KVHEADS * HDIM), 1.0, 6.0, ((0, 32), (2, 8)))
    prompt_lengths = draw_prompt_lengths(jax.random.fold_in(streams_of[14], 71), 0)
    completion_prompt = draw_completion_prompt(jax.random.fold_in(streams_of[14], 71), 0)
    completion_lengths = draw_completion_lengths(jax.random.fold_in(streams_of[14], 71), 0)
    targets = plant(jax.random.randint(streams_of[8], (ROWS_ALL,), 0, VOCAB), jax.random.fold_in(streams_of[8], 1), 0, VOCAB - 1).astype(jnp.int32)
    advantages = scatter_about(streams_of[9], (COMPS,), 1.0, 4.0, (), jnp.float32)
    residual = draw_residual(jax.random.fold_in(streams_of[14], 71), 0)
    out_proj = bell_draw_with(streams_of[11], (HEADS * HDIM, D), (HEADS * HDIM // 4) ** -0.5, 0.25, ((0, 8),), (0, 1, 8, 2.0))
    norm_gain = jnp.clip(1.0 + 0.1 * jax.random.normal(streams_of[12], (D,), jnp.float32), 0.5, 1.5)
    embedding = draw_embedding(jax.random.fold_in(streams_of[14], 71), 0)
    return {"queries": queries, "own_keys": own_keys, "own_values": own_values, "prompt_keys": prompt_keys, "prompt_values": prompt_values, "prompt_lengths": prompt_lengths, "completion_prompt": completion_prompt, "completion_lengths": completion_lengths, "targets": targets, "advantages": advantages, "residual": residual, "out_proj": out_proj, "norm_gain": norm_gain, "embedding": embedding}


score_scale = 168.0 ** (-0.5)
norm_epsilon = 1e-06

def attend(queries, key_block, values, visible):
    step_count = queries.shape[0]
    key_heads = key_block.shape[1]
    group_size = queries.shape[1] // key_heads
    query_float = queries.astype(jnp.float32).reshape(step_count, key_heads, group_size, queries.shape[2])
    scores = jnp.einsum('tkgd,nkd->tkgn', query_float, key_block.astype(jnp.float32)) * score_scale
    scores = jnp.where(visible[:, None, None, :], scores, -jnp.inf)
    row_top = lax.optimization_barrier(jnp.max(scores, axis=-1, keepdims=True))
    exp_scores = jnp.exp(scores - row_top)
    weights = (exp_scores / lax.optimization_barrier(jnp.sum(exp_scores, axis=-1, keepdims=True))).astype(jnp.bfloat16)
    mixed_values = jnp.einsum('tkgn,nkd->tkgd', weights.astype(jnp.float32), values.astype(jnp.float32))
    return mixed_values.reshape(step_count, -1).astype(jnp.bfloat16)

def reference(queries, own_keys, own_values, prompt_keys, prompt_values, prompt_lengths, completion_prompt, completion_lengths, targets, advantages, residual, out_proj, norm_gain, embedding):
    causal = jnp.arange(CLEN)[:, None] >= jnp.arange(CLEN)[None, :]

    def per_completion(members):
        query_rows, key_rows, value_rows, prompt = members
        key_block = jnp.concatenate([prompt_keys[prompt], key_rows], axis=0).reshape(PLEN + CLEN, KVHEADS, HDIM)
        value_block = jnp.concatenate([prompt_values[prompt], value_rows], axis=0).reshape(PLEN + CLEN, KVHEADS, HDIM)
        inside = jnp.arange(PLEN) < prompt_lengths[prompt]
        visible = jnp.concatenate([jnp.broadcast_to(inside[None, :], (CLEN, PLEN)), causal], axis=1)
        return attend(query_rows.reshape(CLEN, HEADS, HDIM), key_block, value_block, visible)
    attended = lax.map(per_completion, (queries.reshape(COMPS, CLEN, HEADS * HDIM), own_keys.reshape(COMPS, CLEN, KVHEADS * HDIM), own_values.reshape(COMPS, CLEN, KVHEADS * HDIM), completion_prompt))
    attended = attended.reshape(COMPS * CLEN, HEADS * HDIM)
    hidden = residual.astype(jnp.float32) + jnp.dot(attended, out_proj, preferred_element_type=jnp.float32)
    norm_factor = lax.rsqrt(lax.optimization_barrier(jnp.mean(hidden * hidden, axis=-1, keepdims=True)) + norm_epsilon)
    normed = (hidden * norm_factor * norm_gain).astype(jnp.bfloat16)
    logits = jnp.dot(normed, embedding.T, preferred_element_type=jnp.float32)
    row_top = lax.optimization_barrier(jnp.max(logits, axis=-1, keepdims=True))
    row_total = lax.optimization_barrier(jnp.sum(jnp.exp(logits - row_top), axis=-1, keepdims=True))
    log_total = row_top + jnp.log(row_total)
    picked = jnp.take_along_axis(logits, targets[:, None].astype(jnp.int32), axis=1)
    logprob = (picked - log_total)[:, 0]
    row_ids = jnp.arange(COMPS * CLEN, dtype=jnp.int32)
    completion_of = row_ids // CLEN
    position = row_ids - completion_of * CLEN
    live_token = position < completion_lengths[completion_of]
    token_weight = jnp.where(live_token, -advantages[completion_of], jnp.zeros((), jnp.float32))
    target_hit = (jnp.arange(VOCAB, dtype=jnp.int32)[None, :] == targets[:, None]).astype(jnp.float32)
    logit_grad = (token_weight[:, None] * (target_hit - jnp.exp(logits - log_total))).astype(jnp.bfloat16)

    def add_slab(slab_index, running):
        first_entry = (slab_index * VDEV).astype(jnp.int32)
        slab_term = jnp.dot(lax.dynamic_slice_in_dim(logit_grad, first_entry, VDEV, 1), lax.dynamic_slice_in_dim(embedding, first_entry, VDEV, 0), preferred_element_type=jnp.float32)
        slab_term = lax.optimization_barrier(slab_term.astype(jnp.bfloat16)).astype(jnp.float32)
        return running + slab_term
    normed_grad = lax.fori_loop(jnp.int32(0), jnp.int32(N_DP * N_VOCAB), add_slab, jnp.zeros((COMPS * CLEN, D), jnp.float32))
    hidden_grad = norm_gain * norm_factor * normed_grad - hidden * norm_factor ** 3 * lax.optimization_barrier(jnp.mean(norm_gain * normed_grad * hidden, axis=-1, keepdims=True))
    return (logprob, hidden_grad)
```

```python
import jax
import jax.numpy as jnp
from jax import lax
from jax.sharding import Mesh
from jax.sharding import PartitionSpec as P

HDIM = 128
CLEN = 8
XS, YS, CS = 4, 4, 2

score_scale = 168.0 ** (-0.5)
norm_epsilon = 1e-06
SWAP = ((0, 1), (1, 0))


def spread(part, axes):
    count = lax.axis_size(axes)
    copies = jnp.broadcast_to(part[None], (count,) + part.shape)
    return lax.all_to_all(copies, axes, 0, 0, tiled=True)


def summed(rows, axes):
    count = lax.axis_size(axes)
    pieces = rows.reshape(count, rows.shape[0] // count, rows.shape[1])
    arrived = lax.all_to_all(pieces, axes, 0, 0, tiled=True)
    return jnp.sum(arrived.astype(jnp.float32), axis=0)


def attend_local(queries, key_block, value_block, visible):
    comp_count, step_count, heads_here, head_width = queries.shape
    key_heads = key_block.shape[2]
    group_size = heads_here // key_heads
    grouped = queries.reshape(comp_count, step_count, key_heads, group_size, head_width)
    scores = (
        jnp.einsum("ctkgd,cnkd->ctkgn", grouped, key_block, preferred_element_type=jnp.float32)
        * score_scale
    )
    scores = jnp.where(visible[:, :, None, None, :], scores, -jnp.inf)
    row_top = jnp.max(scores, axis=-1, keepdims=True)
    exp_scores = jnp.exp(scores - row_top)
    weights = (exp_scores / jnp.sum(exp_scores, axis=-1, keepdims=True)).astype(jnp.bfloat16)
    mixed_values = jnp.einsum(
        "ctkgn,cnkd->ctkgd", weights, value_block, preferred_element_type=jnp.float32
    )
    return mixed_values.reshape(comp_count * step_count, heads_here * head_width).astype(
        jnp.bfloat16
    )


def merged(stats):
    top = jnp.max(stats[:, 0], axis=0)
    total = jnp.sum(stats[:, 1] * jnp.exp(stats[:, 0] - top[None]), axis=0)
    return jnp.stack([top, total, jnp.sum(stats[:, 2], axis=0)])


def body(
    queries,
    own_keys,
    own_values,
    prompt_keys,
    prompt_values,
    prompt_lengths,
    completion_prompt,
    completion_lengths,
    targets,
    advantages,
    residual,
    out_proj,
    norm_gain,
    embedding,
):
    row_count, width = residual.shape
    comp_count = row_count // CLEN
    heads_here = queries.shape[1] // HDIM
    key_heads = own_keys.shape[1] // HDIM
    prompt_span = prompt_keys.shape[1]
    vocab_slab = embedding.shape[0]
    core = lax.axis_index("c")
    plane = lax.axis_index(("x", "y"))
    planes = XS * YS
    layer = lax.axis_index("z")
    layers = lax.axis_size("z")
    dp_index = plane * CS + core

    other_slab = lax.ppermute(embedding, "c", SWAP)

    held = jnp.concatenate([prompt_keys[0], prompt_values[0]], axis=1)
    arrived = spread(held, ("x", "y"))
    by_device = completion_prompt.reshape(planes * CS, comp_count)
    my_prompts = by_device[dp_index]
    partner_prompts = by_device[plane * CS + (1 - core)]
    mine = arrived[my_prompts // CS]
    for_partner = arrived[partner_prompts // CS]
    from_partner = lax.ppermute(for_partner, "c", SWAP)
    here = (my_prompts % CS) == core
    chosen = jnp.where(here[:, None, None], mine, from_partner)
    half = chosen.shape[2] // 2
    key_block = jnp.concatenate([chosen[:, :, :half], own_keys.reshape(comp_count, CLEN, -1)], axis=1)
    key_block = key_block.reshape(comp_count, prompt_span + CLEN, key_heads, HDIM)
    value_block = jnp.concatenate(
        [chosen[:, :, half:], own_values.reshape(comp_count, CLEN, -1)], axis=1
    )
    value_block = value_block.reshape(comp_count, prompt_span + CLEN, key_heads, HDIM)
    inside = jnp.arange(prompt_span)[None, :] < prompt_lengths[my_prompts][:, None]
    causal = jnp.arange(CLEN)[:, None] >= jnp.arange(CLEN)[None, :]
    visible = jnp.concatenate(
        [
            jnp.broadcast_to(inside[:, None, :], (comp_count, CLEN, prompt_span)),
            jnp.broadcast_to(causal[None], (comp_count, CLEN, CLEN)),
        ],
        axis=2,
    )
    attended = attend_local(
        queries.reshape(comp_count, CLEN, heads_here, HDIM), key_block, value_block, visible
    )
    partial_value = jnp.dot(attended, out_proj, preferred_element_type=jnp.float32)

    share = row_count // layers
    head_total = summed(partial_value, "z")
    my_residual = lax.dynamic_slice_in_dim(residual, layer * share, share)
    hidden = my_residual.astype(jnp.float32) + head_total
    norm_factor = lax.rsqrt(jnp.mean(hidden * hidden, axis=-1, keepdims=True) + norm_epsilon)
    normed = (hidden * norm_factor * norm_gain).astype(jnp.bfloat16)

    normed = spread(normed, "z").reshape(row_count, width)
    every_row = lax.all_gather(normed, ("x", "y"), axis=0, tiled=True)
    rows_here = planes * row_count

    contract_last = (((1,), (1,)), ((), ()))
    logits = [
        lax.dot_general(every_row, slab, contract_last, preferred_element_type=jnp.float32)
        for slab in (embedding, other_slab)
    ]
    my_targets = targets.reshape(planes, CS, row_count)[:, core].reshape(rows_here)
    column_ids = jnp.arange(vocab_slab, dtype=jnp.int32)
    hits = []
    for which in (core, 1 - core):
        slab_index = (plane * CS + which) * layers + layer
        local_target = my_targets - slab_index * vocab_slab
        hits.append(column_ids[None, :] == local_target[:, None])
    top = jnp.maximum(jnp.max(logits[0], axis=1), jnp.max(logits[1], axis=1))
    total = sum(jnp.sum(jnp.exp(part - top[:, None]), axis=1) for part in logits)
    picked = sum(jnp.sum(jnp.where(hit, part, 0.0), axis=1) for hit, part in zip(hits, logits))
    stats = jnp.stack([top, total, picked])
    stats = merged(spread(stats, "z"))
    stats = merged(spread(stats, ("x", "y")))
    log_total = stats[0] + jnp.log(stats[1])
    logprob = lax.dynamic_slice_in_dim(stats[2] - log_total, plane * row_count, row_count)

    position = jnp.arange(row_count, dtype=jnp.int32) % CLEN
    live_token = position[None, :] < jnp.repeat(
        completion_lengths.reshape(planes * CS, comp_count), CLEN, axis=1
    )
    weight_of = jnp.where(
        live_token, -jnp.repeat(advantages.reshape(planes * CS, comp_count), CLEN, axis=1), 0.0
    )
    token_weight = weight_of.reshape(planes, CS, row_count)[:, core].reshape(rows_here)
    grads = [
        (
            token_weight[:, None] * (hit.astype(jnp.float32) - jnp.exp(part - log_total[:, None]))
        ).astype(jnp.bfloat16)
        for hit, part in zip(hits, logits)
    ]
    terms = jnp.dot(grads[0], embedding, preferred_element_type=jnp.float32) + jnp.dot(
        grads[1], other_slab, preferred_element_type=jnp.float32
    )
    summed_rows = summed(terms.astype(jnp.bfloat16), ("x", "y"))
    normed_grad = summed(summed_rows, "z")
    hidden_grad = norm_gain * norm_factor * normed_grad - hidden * norm_factor**3 * jnp.mean(
        norm_gain * normed_grad * hidden, axis=-1, keepdims=True
    )
    hidden_grad = spread(hidden_grad, "z").reshape(row_count, width)
    return (logprob, hidden_grad)


def solution(mesh):
    fine = Mesh(mesh.devices.reshape(XS, YS, CS, -1), ("x", "y", "c", "z"))
    dp = ("x", "y", "c")
    placed = (
        P(dp, "z"),
        P(dp, "z"),
        P(dp, "z"),
        P(dp, None, "z"),
        P(dp, None, "z"),
        P(),
        P(),
        P(),
        P(),
        P(),
        P(dp, None),
        P("z", None),
        P(),
        P(dp + ("z",), None),
    )
    return jax.shard_map(
        body, mesh=fine, in_specs=placed, out_specs=(P(dp), P(dp, None)), check_vma=False
    )
```

```python
import jax
import jax.numpy as jnp
from jax import lax
from jax.sharding import Mesh
from jax.sharding import PartitionSpec as P

HDIM = 128
CLEN = 8
XS, YS, CS = 4, 4, 2

score_scale = 168.0 ** (-0.5)
norm_epsilon = 1e-06
SWAP = ((0, 1), (1, 0))
Z = ("zh", "zl")


def spread(part, axes):
    count = lax.axis_size(axes)
    copies = jnp.broadcast_to(part[None], (count,) + part.shape)
    return lax.all_to_all(copies, axes, 0, 0, tiled=True)


def summed(rows, axes):
    count = lax.axis_size(axes)
    pieces = rows.reshape(count, rows.shape[0] // count, rows.shape[1])
    arrived = lax.all_to_all(pieces, axes, 0, 0, tiled=True)
    return jnp.sum(arrived.astype(jnp.float32), axis=0)


def attend_local(queries, key_block, value_block, visible):
    comp_count, step_count, heads_here, head_width = queries.shape
    key_heads = key_block.shape[2]
    group_size = heads_here // key_heads
    grouped = queries.reshape(comp_count, step_count, key_heads, group_size, head_width)
    scores = (
        jnp.einsum("ctkgd,cnkd->ctkgn", grouped, key_block, preferred_element_type=jnp.float32)
        * score_scale
    )
    scores = jnp.where(visible[:, :, None, None, :], scores, -jnp.inf)
    row_top = jnp.max(scores, axis=-1, keepdims=True)
    exp_scores = jnp.exp(scores - row_top)
    weights = (exp_scores / jnp.sum(exp_scores, axis=-1, keepdims=True)).astype(jnp.bfloat16)
    mixed_values = jnp.einsum(
        "ctkgn,cnkd->ctkgd", weights, value_block, preferred_element_type=jnp.float32
    )
    return mixed_values.reshape(comp_count * step_count, heads_here * head_width).astype(
        jnp.bfloat16
    )


def merged(stats):
    top = jnp.max(stats[:, 0], axis=0)
    total = jnp.sum(stats[:, 1] * jnp.exp(stats[:, 0] - top[None]), axis=0)
    return jnp.stack([top, total, jnp.sum(stats[:, 2], axis=0)])


def body(
    queries,
    own_keys,
    own_values,
    prompt_keys,
    prompt_values,
    prompt_lengths,
    completion_prompt,
    completion_lengths,
    targets,
    advantages,
    residual,
    out_proj,
    norm_gain,
    embedding,
):
    row_count, width = residual.shape
    comp_count = row_count // CLEN
    heads_here = queries.shape[1] // HDIM
    key_heads = own_keys.shape[1] // HDIM
    prompt_span = prompt_keys.shape[1]
    vocab_slab = embedding.shape[0]
    core = lax.axis_index("c")
    plane = lax.axis_index(("x", "y"))
    planes = XS * YS
    layer = lax.axis_index(Z)
    layers = lax.axis_size(Z)
    parity = lax.axis_index("zl")
    dp_index = plane * CS + core

    half_slab = vocab_slab // 2
    ring = range(layers)
    from_next = lax.ppermute(embedding[:half_slab], Z, [((k + 1) % layers, k) for k in ring])
    from_prev = lax.ppermute(embedding[half_slab:], Z, [(k, (k + 1) % layers) for k in ring])
    near = jnp.concatenate([from_next, from_prev], axis=0)
    table = jnp.concatenate(
        [embedding, lax.ppermute(embedding, "c", SWAP), near, lax.ppermute(near, "c", SWAP)], axis=0
    )
    slab_column = jnp.arange(vocab_slab, dtype=jnp.int32)
    near_layer = jnp.where(slab_column < half_slab, layer + 1, layer - 1) % layers
    entry = jnp.concatenate(
        [
            ((plane * CS + which) * layers + held_layer) * vocab_slab + slab_column
            for held_layer in (layer, near_layer)
            for which in (core, 1 - core)
        ]
    )

    held = jnp.concatenate([prompt_keys[0], prompt_values[0]], axis=1)
    arrived = spread(held, ("x", "y"))
    by_device = completion_prompt.reshape(planes * CS, comp_count)
    my_prompts = by_device[dp_index]
    partner_prompts = by_device[plane * CS + (1 - core)]
    mine = arrived[my_prompts // CS]
    for_partner = arrived[partner_prompts // CS]
    from_partner = lax.ppermute(for_partner, "c", SWAP)
    here = (my_prompts % CS) == core
    chosen = jnp.where(here[:, None, None], mine, from_partner)
    half = chosen.shape[2] // 2
    key_block = jnp.concatenate([chosen[:, :, :half], own_keys.reshape(comp_count, CLEN, -1)], axis=1)
    key_block = key_block.reshape(comp_count, prompt_span + CLEN, key_heads, HDIM)
    value_block = jnp.concatenate(
        [chosen[:, :, half:], own_values.reshape(comp_count, CLEN, -1)], axis=1
    )
    value_block = value_block.reshape(comp_count, prompt_span + CLEN, key_heads, HDIM)
    inside = jnp.arange(prompt_span)[None, :] < prompt_lengths[my_prompts][:, None]
    causal = jnp.arange(CLEN)[:, None] >= jnp.arange(CLEN)[None, :]
    visible = jnp.concatenate(
        [
            jnp.broadcast_to(inside[:, None, :], (comp_count, CLEN, prompt_span)),
            jnp.broadcast_to(causal[None], (comp_count, CLEN, CLEN)),
        ],
        axis=2,
    )
    attended = attend_local(
        queries.reshape(comp_count, CLEN, heads_here, HDIM), key_block, value_block, visible
    )
    partial_value = jnp.dot(attended, out_proj, preferred_element_type=jnp.float32)

    share = row_count // layers
    head_total = summed(partial_value, Z)
    my_residual = lax.dynamic_slice_in_dim(residual, layer * share, share)
    hidden = my_residual.astype(jnp.float32) + head_total
    norm_factor = lax.rsqrt(jnp.mean(hidden * hidden, axis=-1, keepdims=True) + norm_epsilon)
    normed = (hidden * norm_factor * norm_gain).astype(jnp.bfloat16)

    pairs = layers // 2
    normed = spread(normed, "zh").reshape(pairs * share, width)
    rows_here = planes * pairs * share
    every_row = spread(normed, ("x", "y")).reshape(rows_here, width)

    def of_rows(values):
        return values.reshape(planes, CS, pairs, 2, share)[:, core, :, parity].reshape(rows_here)

    logits = lax.dot_general(
        every_row, table, (((1,), (1,)), ((), ())), preferred_element_type=jnp.float32
    )
    hit = entry[None, :] == of_rows(targets)[:, None]
    top = jnp.max(logits, axis=1)
    total = jnp.sum(jnp.exp(logits - top[:, None]), axis=1)
    picked = jnp.sum(jnp.where(hit, logits, 0.0), axis=1)
    stats = jnp.stack([top, total, picked])
    stats = merged(spread(stats, "zh"))
    stats = merged(spread(stats, ("x", "y")))
    log_total = stats[0] + jnp.log(stats[1])
    first_row = (plane * pairs + lax.axis_index("zh")) * share
    logprob = lax.dynamic_slice_in_dim(stats[2] - log_total, first_row, share)
    logprob = spread(logprob, Z).reshape(row_count)

    row_ids = jnp.arange(targets.shape[0], dtype=jnp.int32)
    live_token = row_ids % CLEN < jnp.repeat(completion_lengths, CLEN)
    token_weight = of_rows(jnp.where(live_token, -jnp.repeat(advantages, CLEN), 0.0))
    logit_grad = (
        token_weight[:, None] * (hit.astype(jnp.float32) - jnp.exp(logits - log_total[:, None]))
    ).astype(jnp.bfloat16)
    terms = jnp.dot(logit_grad, table, preferred_element_type=jnp.float32)
    summed_rows = summed(terms.astype(jnp.bfloat16), ("x", "y"))
    normed_grad = summed(summed_rows, "zh")
    hidden_grad = norm_gain * norm_factor * normed_grad - hidden * norm_factor**3 * jnp.mean(
        norm_gain * normed_grad * hidden, axis=-1, keepdims=True
    )
    hidden_grad = spread(hidden_grad.astype(jnp.bfloat16), Z).reshape(row_count, width)
    return (logprob, hidden_grad.astype(jnp.float32))


def solution(mesh):
    fine = Mesh(mesh.devices.reshape(XS, YS, CS, -1, 2), ("x", "y", "c") + Z)
    dp = ("x", "y", "c")
    placed = (
        P(dp, Z),
        P(dp, Z),
        P(dp, Z),
        P(dp, None, Z),
        P(dp, None, Z),
        P(),
        P(),
        P(),
        P(),
        P(),
        P(dp, None),
        P(Z, None),
        P(),
        P(dp + Z, None),
    )
    return jax.shard_map(
        body, mesh=fine, in_specs=placed, out_specs=(P(dp), P(dp, None)), check_vma=False
    )
```

```python
import jax
import jax.numpy as jnp
from jax import lax
from jax.experimental import pallas as pl
from jax.experimental.pallas import tpu as pltpu
from jax.sharding import Mesh
from jax.sharding import PartitionSpec as P

HDIM = 128
CLEN = 8
XS, YS, CS = 4, 4, 2

score_scale = 168.0 ** (-0.5)
norm_epsilon = 1e-06
SWAP = ((0, 1), (1, 0))
Z = ("zh", "zl")


def spread(part, axes):
    count = lax.axis_size(axes)
    copies = jnp.broadcast_to(part[None], (count,) + part.shape)
    return lax.all_to_all(copies, axes, 0, 0, tiled=True)


def summed(rows, axes):
    count = lax.axis_size(axes)
    pieces = rows.reshape(count, rows.shape[0] // count, rows.shape[1])
    arrived = lax.all_to_all(pieces, axes, 0, 0, tiled=True)
    return jnp.sum(arrived.astype(jnp.float32), axis=0)


def attend_local(queries, key_block, value_block, visible):
    comp_count, step_count, heads_here, head_width = queries.shape
    key_heads = key_block.shape[2]
    group_size = heads_here // key_heads
    grouped = queries.reshape(comp_count, step_count, key_heads, group_size, head_width)
    scores = (
        jnp.einsum("ctkgd,cnkd->ctkgn", grouped, key_block, preferred_element_type=jnp.float32)
        * score_scale
    )
    scores = jnp.where(visible[:, :, None, None, :], scores, -jnp.inf)
    row_top = jnp.max(scores, axis=-1, keepdims=True)
    exp_scores = jnp.exp(scores - row_top)
    weights = (exp_scores / jnp.sum(exp_scores, axis=-1, keepdims=True)).astype(jnp.bfloat16)
    mixed_values = jnp.einsum(
        "ctkgn,cnkd->ctkgd", weights, value_block, preferred_element_type=jnp.float32
    )
    return mixed_values.reshape(comp_count * step_count, heads_here * head_width).astype(
        jnp.bfloat16
    )


def merged(stats):
    top = jnp.max(stats[:, 0], axis=0)
    total = jnp.sum(stats[:, 1] * jnp.exp(stats[:, 0] - top[None]), axis=0)
    return jnp.stack([top, total, jnp.sum(stats[:, 2], axis=0)])


NT = (((1,), (1,)), ((), ()))
VMEM_BYTES = 44 * 1024 * 1024


def logits_kernel(rows, target_column, *refs):
    slabs, (logits, stats, held, arrivals) = refs[:4], refs[4:]
    depth = held.shape[1]
    chunk = depth // 2
    steps = [(k, part) for k in range(len(slabs)) for part in range(2)]
    copies = [
        pltpu.make_async_copy(
            slabs[k].at[pl.ds(part * chunk, chunk)],
            held.at[k, pl.ds(part * chunk, chunk)],
            arrivals.at[2 * k + part],
        )
        for k, part in steps
    ]
    for copy in copies:
        copy.start()
    top = None
    for (k, part), copy in zip(steps, copies):
        copy.wait()
        block = lax.dot_general(
            held[k, pl.ds(part * chunk, chunk), :],
            rows[...],
            NT,
            preferred_element_type=jnp.float32,
        )
        logits[pl.ds(k * depth + part * chunk, chunk), :] = block
        block_top = jnp.max(block, axis=0, keepdims=True)
        top = block_top if top is None else jnp.maximum(top, block_top)
    total = jnp.zeros_like(top)
    picked = jnp.zeros_like(top)
    for k, part in steps:
        start = k * depth + part * chunk
        block = logits[pl.ds(start, chunk), :]
        hit = lax.broadcasted_iota(jnp.int32, block.shape, 0) + start == target_column[...]
        total += jnp.sum(jnp.exp(block - top), axis=0, keepdims=True)
        picked += jnp.sum(jnp.where(hit, block, 0.0), axis=0, keepdims=True)
    line = lax.broadcasted_iota(jnp.int32, stats.shape, 0)
    stats[...] = jnp.where(line == 0, top, jnp.where(line == 1, total, picked))


def gradient_kernel(logits, target_column, log_total, token_weight, *refs):
    slabs, (terms, grad) = refs[:4], refs[4:]
    depth = slabs[0].shape[0]
    chunk = depth // 2

    @pl.when(pl.program_id(0) == 0)
    def _():
        for start in range(0, len(slabs) * depth, chunk):
            block = logits[pl.ds(start, chunk), :]
            hit = lax.broadcasted_iota(jnp.int32, block.shape, 0) + start == target_column[...]
            block = jnp.where(hit, 1.0, 0.0) - jnp.exp(block - log_total[...])
            grad[:, pl.ds(start, chunk)] = (token_weight[...] * block).T.astype(jnp.bfloat16)

    sums = [
        jnp.dot(
            grad[:, pl.ds(k * depth, depth)], slab[...], preferred_element_type=jnp.float32
        )
        for k, slab in enumerate(slabs)
    ]
    terms[...] = ((sums[0] + sums[1]) + (sums[2] + sums[3])).astype(jnp.bfloat16)


def slab_logits(rows, target_column, slabs):
    depth, width = slabs[0].shape
    count, entries = rows.shape[0], depth * len(slabs)
    whole = pl.BlockSpec(memory_space=pltpu.VMEM)
    return pl.pallas_call(
        logits_kernel,
        out_shape=(
            jax.ShapeDtypeStruct((entries, count), jnp.float32),
            jax.ShapeDtypeStruct((8, count), jnp.float32),
        ),
        in_specs=[whole, whole] + [pl.BlockSpec(memory_space=pl.ANY)] * len(slabs),
        out_specs=[whole, whole],
        scratch_shapes=[
            pltpu.VMEM((len(slabs), depth, width), jnp.bfloat16),
            pltpu.SemaphoreType.DMA((2 * len(slabs),)),
        ],
        compiler_params=pltpu.CompilerParams(vmem_limit_bytes=VMEM_BYTES),
        cost_estimate=pl.CostEstimate(
            flops=2 * count * entries * width,
            bytes_accessed=2 * entries * width,
            transcendentals=count * entries,
        ),
    )(rows, target_column, *slabs)


def slab_gradient(logits, target_column, log_total, token_weight, slabs):
    depth, width = slabs[0].shape
    entries, count = logits.shape
    tile = next(t for t in (768, 512, 256, 128) if width % t == 0)

    def fixed(shape):
        return pl.BlockSpec(shape, lambda i: (0, 0))

    return pl.pallas_call(
        gradient_kernel,
        grid=(width // tile,),
        out_shape=jax.ShapeDtypeStruct((count, width), jnp.bfloat16),
        in_specs=[fixed((entries, count))]
        + [fixed((1, count))] * 3
        + [pl.BlockSpec((depth, tile), lambda i: (0, i))] * len(slabs),
        out_specs=pl.BlockSpec((count, tile), lambda i: (0, i)),
        scratch_shapes=[pltpu.VMEM((count, entries), jnp.bfloat16)],
        compiler_params=pltpu.CompilerParams(vmem_limit_bytes=VMEM_BYTES),
        cost_estimate=pl.CostEstimate(
            flops=2 * count * entries * width,
            bytes_accessed=2 * entries * width,
            transcendentals=count * entries,
        ),
    )(logits, target_column, log_total, token_weight, *slabs)


def body(
    queries,
    own_keys,
    own_values,
    prompt_keys,
    prompt_values,
    prompt_lengths,
    completion_prompt,
    completion_lengths,
    targets,
    advantages,
    residual,
    out_proj,
    norm_gain,
    embedding,
):
    row_count, width = residual.shape
    comp_count = row_count // CLEN
    heads_here = queries.shape[1] // HDIM
    key_heads = own_keys.shape[1] // HDIM
    prompt_span = prompt_keys.shape[1]
    vocab_slab = embedding.shape[0]
    core = lax.axis_index("c")
    plane = lax.axis_index(("x", "y"))
    planes = XS * YS
    layer = lax.axis_index(Z)
    layers = lax.axis_size(Z)
    odd_layer = lax.axis_index("zl")
    odd_x = lax.axis_index("x") % 2
    parity = (odd_x + odd_layer) % 2
    dp_index = plane * CS + core

    quarter = vocab_slab // 4

    def from_neighbour(part, axes, ahead):
        size = lax.axis_size(axes)
        pairs = [((k + ahead) % size, k) for k in range(size)]
        return lax.ppermute(embedding[part * quarter : (part + 1) * quarter], axes, pairs)

    pieces = (
        from_neighbour(0, Z, 1),
        from_neighbour(1, Z, -1),
        from_neighbour(2, "x", 1),
        from_neighbour(3, "x", -1),
    )
    across = lax.ppermute(embedding, "c", SWAP)
    along_x = lax.axis_index("x")
    slab_column = jnp.arange(vocab_slab, dtype=jnp.int32)
    near_layer = jnp.where(slab_column < quarter, layer + 1, layer)
    near_layer = jnp.where(slab_column // quarter == 1, layer - 1, near_layer) % layers
    near_x = jnp.where(slab_column // quarter == 2, along_x + 1, along_x)
    near_x = jnp.where(slab_column // quarter == 3, along_x - 1, near_x) % XS
    near_plane = near_x * YS + lax.axis_index("y")
    entry = jnp.concatenate(
        [
            ((at_plane * CS + which) * layers + at_layer) * vocab_slab + slab_column
            for at_plane, at_layer in ((plane, layer), (near_plane, near_layer))
            for which in (core, 1 - core)
        ]
    )

    held = jnp.concatenate([prompt_keys[0], prompt_values[0]], axis=1)
    arrived = spread(held, ("x", "y"))
    by_device = completion_prompt.reshape(planes * CS, comp_count)
    my_prompts = by_device[dp_index]
    partner_prompts = by_device[plane * CS + (1 - core)]
    mine = arrived[my_prompts // CS]
    for_partner = arrived[partner_prompts // CS]
    from_partner = lax.ppermute(for_partner, "c", SWAP)
    here = (my_prompts % CS) == core
    chosen = jnp.where(here[:, None, None], mine, from_partner)
    half = chosen.shape[2] // 2
    key_block = jnp.concatenate([chosen[:, :, :half], own_keys.reshape(comp_count, CLEN, -1)], axis=1)
    key_block = key_block.reshape(comp_count, prompt_span + CLEN, key_heads, HDIM)
    value_block = jnp.concatenate(
        [chosen[:, :, half:], own_values.reshape(comp_count, CLEN, -1)], axis=1
    )
    value_block = value_block.reshape(comp_count, prompt_span + CLEN, key_heads, HDIM)
    inside = jnp.arange(prompt_span)[None, :] < prompt_lengths[my_prompts][:, None]
    causal = jnp.arange(CLEN)[:, None] >= jnp.arange(CLEN)[None, :]
    visible = jnp.concatenate(
        [
            jnp.broadcast_to(inside[:, None, :], (comp_count, CLEN, prompt_span)),
            jnp.broadcast_to(causal[None], (comp_count, CLEN, CLEN)),
        ],
        axis=2,
    )
    attended = attend_local(
        queries.reshape(comp_count, CLEN, heads_here, HDIM), key_block, value_block, visible
    )
    partial_value = jnp.dot(attended, out_proj, preferred_element_type=jnp.float32)

    partial_value, pieces, across = lax.optimization_barrier((partial_value, pieces, across))
    near = jnp.concatenate(pieces, axis=0)
    near_across = lax.ppermute(near, "c", SWAP)

    share = row_count // layers
    head_total = summed(partial_value, Z)
    head_total, near_across = lax.optimization_barrier((head_total, near_across))
    slabs = (embedding, across, near, near_across)
    my_residual = lax.dynamic_slice_in_dim(residual, layer * share, share)
    hidden = my_residual.astype(jnp.float32) + head_total
    norm_factor = lax.rsqrt(jnp.mean(hidden * hidden, axis=-1, keepdims=True) + norm_epsilon)
    normed = (hidden * norm_factor * norm_gain).astype(jnp.bfloat16)

    pairs = layers // 2
    by_parity = spread(normed, Z).reshape(pairs, 2, share, width).transpose(1, 0, 2, 3)
    by_parity = by_parity.reshape(2, pairs * share, width)
    rows_here = planes * pairs * share
    for_even_x = jnp.where(odd_layer == 0, by_parity[0], by_parity[1])
    for_odd_x = jnp.where(odd_layer == 0, by_parity[1], by_parity[0])
    to_odd_x = (jnp.arange(planes) // YS % 2 == 1)[:, None, None]
    outgoing = jnp.where(to_odd_x, for_odd_x[None], for_even_x[None])
    every_row = lax.all_to_all(outgoing, ("x", "y"), 0, 0, tiled=True).reshape(rows_here, width)

    def of_rows(values):
        return values.reshape(planes, CS, pairs, 2, share)[:, core, :, parity].reshape(rows_here)

    def even_first(both, odd):
        return jnp.where(odd == 0, both, both[::-1])

    hit = entry[:, None] == of_rows(targets)[None, :]
    numbers = jnp.arange(entry.shape[0], dtype=jnp.int32)[:, None]
    target_column = jnp.max(jnp.where(hit, numbers, -1), axis=0, keepdims=True)
    logits, stats = slab_logits(every_row, target_column, slabs)
    column = spread(stats[:3], Z).reshape(pairs, 2, 3, rows_here)
    column = even_first(jnp.stack([merged(column[:, 0]), merged(column[:, 1])]), odd_x)
    stats = spread(column, ("x", "y"))
    stats = jnp.stack([merged(stats[:, 0]), merged(stats[:, 1])])
    log_total = stats[:, 0] + jnp.log(stats[:, 1])
    every_logprob = (stats[:, 2] - log_total).reshape(2, planes, pairs, share)
    logprob = every_logprob[:, plane].transpose(1, 0, 2).reshape(row_count)

    row_ids = jnp.arange(targets.shape[0], dtype=jnp.int32)
    live_token = row_ids % CLEN < jnp.repeat(completion_lengths, CLEN)
    token_weight = of_rows(jnp.where(live_token, -jnp.repeat(advantages, CLEN), 0.0))
    terms = slab_gradient(
        logits, target_column, log_total[parity][None], token_weight[None], slabs
    )
    arrived = lax.all_to_all(
        terms.reshape(planes, pairs * share, width), ("x", "y"), 0, 0, tiled=True
    )
    arrived = arrived.reshape(XS // 2, 2, YS, pairs * share, width).astype(jnp.float32)
    both = even_first(jnp.sum(arrived, axis=(0, 2)), odd_layer)
    both = both.reshape(2, pairs, share, width).transpose(1, 0, 2, 3).reshape(row_count, width)
    normed_grad = summed(both.astype(jnp.bfloat16), Z)
    hidden_grad = norm_gain * norm_factor * normed_grad - hidden * norm_factor**3 * jnp.mean(
        norm_gain * normed_grad * hidden, axis=-1, keepdims=True
    )
    hidden_grad = spread(hidden_grad.astype(jnp.bfloat16), Z).reshape(row_count, width)
    return (logprob, hidden_grad.astype(jnp.float32))


def solution(mesh):
    fine = Mesh(mesh.devices.reshape(XS, YS, CS, -1, 2), ("x", "y", "c") + Z)
    dp = ("x", "y", "c")
    placed = (
        P(dp, Z),
        P(dp, Z),
        P(dp, Z),
        P(dp, None, Z),
        P(dp, None, Z),
        P(),
        P(),
        P(),
        P(),
        P(),
        P(dp, None),
        P(Z, None),
        P(),
        P(dp + Z, None),
    )
    return jax.shard_map(
        body, mesh=fine, in_specs=placed, out_specs=(P(dp), P(dp, None)), check_vma=False
    )
```

```python
import jax
import jax.numpy as jnp
from jax import lax
from jax.experimental import pallas as pl
from jax.experimental.pallas import tpu as pltpu
from jax.sharding import Mesh
from jax.sharding import PartitionSpec as P

HDIM = 128
CLEN = 8
XS, YS, CS = 4, 4, 2

score_scale = 168.0 ** (-0.5)
norm_epsilon = 1e-06
SWAP = ((0, 1), (1, 0))
Z = ("zh", "zl")


def spread(part, axes):
    count = lax.axis_size(axes)
    copies = jnp.broadcast_to(part[None], (count,) + part.shape)
    return lax.all_to_all(copies, axes, 0, 0, tiled=True)


def summed(rows, axes):
    count = lax.axis_size(axes)
    pieces = rows.reshape(count, rows.shape[0] // count, rows.shape[1])
    arrived = lax.all_to_all(pieces, axes, 0, 0, tiled=True)
    return jnp.sum(arrived.astype(jnp.float32), axis=0)


def attend_local(queries, key_block, value_block, visible):
    comp_count, step_count, heads_here, head_width = queries.shape
    key_heads = key_block.shape[2]
    group_size = heads_here // key_heads
    grouped = queries.reshape(comp_count, step_count, key_heads, group_size, head_width)
    scores = (
        jnp.einsum("ctkgd,cnkd->ctkgn", grouped, key_block, preferred_element_type=jnp.float32)
        * score_scale
    )
    scores = jnp.where(visible[:, :, None, None, :], scores, -jnp.inf)
    row_top = jnp.max(scores, axis=-1, keepdims=True)
    exp_scores = jnp.exp(scores - row_top)
    weights = (exp_scores / jnp.sum(exp_scores, axis=-1, keepdims=True)).astype(jnp.bfloat16)
    mixed_values = jnp.einsum(
        "ctkgn,cnkd->ctkgd", weights, value_block, preferred_element_type=jnp.float32
    )
    return mixed_values.reshape(comp_count * step_count, heads_here * head_width).astype(
        jnp.bfloat16
    )


def merged(stats):
    top = jnp.max(stats[:, 0], axis=0)
    total = jnp.sum(stats[:, 1] * jnp.exp(stats[:, 0] - top[None]), axis=0)
    return jnp.stack([top, total, jnp.sum(stats[:, 2], axis=0)])


NT = (((1,), (1,)), ((), ()))


def join_kernel(*refs):
    parts, (whole, arrivals) = refs[:-2], refs[-2:]
    depth = parts[0].shape[0]
    copies = [
        pltpu.make_async_copy(part, whole.at[pl.ds(k * depth, depth)], arrivals.at[k])
        for k, part in enumerate(parts)
    ]
    for copy in copies:
        copy.start()
    for copy in copies:
        copy.wait()


def join(parts):
    depth, width = parts[0].shape
    anywhere = pl.BlockSpec(memory_space=pl.ANY)
    return pl.pallas_call(
        join_kernel,
        out_shape=jax.ShapeDtypeStruct((depth * len(parts), width), parts[0].dtype),
        in_specs=[anywhere] * len(parts),
        out_specs=anywhere,
        scratch_shapes=[pltpu.SemaphoreType.DMA((len(parts),))],
    )(*parts)


def logits_kernel(rows, target_column, *refs):
    slabs, (logits, stats, held, held_rows, arrivals, rows_arrival) = refs[:4], refs[4:]
    depth = held.shape[1]
    half = depth // 2
    rows_copy = pltpu.make_async_copy(rows, held_rows, rows_arrival)
    rows_copy.start()
    copies = [
        pltpu.make_async_copy(
            slab.at[pl.ds(start, half)], held.at[k, pl.ds(start, half)], arrivals.at[k, part]
        )
        for k, slab in enumerate(slabs)
        for part, start in enumerate((0, half))
    ]
    for copy in copies:
        copy.start()
    rows_copy.wait()
    top = total = picked = None
    for k in range(len(slabs)):
        copies[2 * k].wait()
        copies[2 * k + 1].wait()
        block = lax.dot_general(
            held[k], held_rows[...], NT, preferred_element_type=jnp.float32
        )
        logits[pl.ds(k * depth, depth), :] = block
        hit = lax.broadcasted_iota(jnp.int32, block.shape, 0) + k * depth == target_column[...]
        block_picked = jnp.sum(jnp.where(hit, block, 0.0), axis=0, keepdims=True)
        block_top = jnp.max(block, axis=0, keepdims=True)
        new_top = block_top if k == 0 else jnp.maximum(top, block_top)
        block_total = jnp.sum(jnp.exp(block - new_top), axis=0, keepdims=True)
        total = block_total if k == 0 else total * jnp.exp(top - new_top) + block_total
        picked = block_picked if k == 0 else picked + block_picked
        top = new_top
    line = lax.broadcasted_iota(jnp.int32, stats.shape, 0)
    stats[...] = jnp.where(line == 0, top, jnp.where(line == 1, total, picked))


def gradient_kernel(logits, target_column, log_total, token_weight, *refs):
    slabs, (terms, grad) = refs[:4], refs[4:]
    depth = slabs[0].shape[0]
    chunk = depth // 2

    @pl.when(pl.program_id(0) == 0)
    def _():
        for start in range(0, len(slabs) * depth, chunk):
            block = logits[pl.ds(start, chunk), :]
            hit = lax.broadcasted_iota(jnp.int32, block.shape, 0) + start == target_column[...]
            block = jnp.where(hit, 1.0, 0.0) - jnp.exp(block - log_total[...])
            grad[:, pl.ds(start, chunk)] = (token_weight[...] * block).T.astype(jnp.bfloat16)

    sums = [
        jnp.dot(
            grad[:, pl.ds(k * depth, depth)], slab[...], preferred_element_type=jnp.float32
        )
        for k, slab in enumerate(slabs)
    ]
    terms[...] = ((sums[0] + sums[1]) + (sums[2] + sums[3])).astype(jnp.bfloat16)


def slab_logits(rows, target_column, slabs):
    depth, width = slabs[0].shape
    count, entries = rows.shape[0], depth * len(slabs)
    whole = pl.BlockSpec(memory_space=pltpu.VMEM)
    anywhere = pl.BlockSpec(memory_space=pl.ANY)
    return pl.pallas_call(
        logits_kernel,
        out_shape=(
            jax.ShapeDtypeStruct((entries, count), jnp.float32),
            jax.ShapeDtypeStruct((8, count), jnp.float32),
        ),
        in_specs=[anywhere, whole] + [anywhere] * len(slabs),
        out_specs=[whole, whole],
        scratch_shapes=[
            pltpu.VMEM((len(slabs), depth, width), jnp.bfloat16),
            pltpu.VMEM((count, width), jnp.bfloat16),
            pltpu.SemaphoreType.DMA((len(slabs), 2)),
            pltpu.SemaphoreType.DMA,
        ],
        compiler_params=pltpu.CompilerParams(vmem_limit_bytes=36 * 1024 * 1024),
        cost_estimate=pl.CostEstimate(
            flops=2 * count * entries * width,
            bytes_accessed=2 * entries * width,
            transcendentals=count * entries,
        ),
    )(rows, target_column, *slabs)


def slab_gradient(logits, target_column, log_total, token_weight, slabs):
    depth, width = slabs[0].shape
    entries, count = logits.shape
    tile = next(t for t in (768, 512, 256, 128) if width % t == 0)

    def fixed(shape):
        return pl.BlockSpec(shape, lambda i: (0, 0))

    return pl.pallas_call(
        gradient_kernel,
        grid=(width // tile,),
        out_shape=jax.ShapeDtypeStruct((count, width), jnp.bfloat16),
        in_specs=[fixed((entries, count))]
        + [fixed((1, count))] * 3
        + [pl.BlockSpec((depth, tile), lambda i: (0, i))] * len(slabs),
        out_specs=pl.BlockSpec((count, tile), lambda i: (0, i)),
        scratch_shapes=[pltpu.VMEM((count, entries), jnp.bfloat16)],
        compiler_params=pltpu.CompilerParams(vmem_limit_bytes=20 * 1024 * 1024),
        cost_estimate=pl.CostEstimate(
            flops=2 * count * entries * width,
            bytes_accessed=2 * entries * width,
            transcendentals=count * entries,
        ),
    )(logits, target_column, log_total, token_weight, *slabs)


def body(
    queries,
    own_keys,
    own_values,
    prompt_keys,
    prompt_values,
    prompt_lengths,
    completion_prompt,
    completion_lengths,
    targets,
    advantages,
    residual,
    out_proj,
    norm_gain,
    embedding,
):
    row_count, width = residual.shape
    comp_count = row_count // CLEN
    heads_here = queries.shape[1] // HDIM
    key_heads = own_keys.shape[1] // HDIM
    prompt_span = prompt_keys.shape[1]
    vocab_slab = embedding.shape[0]
    core = lax.axis_index("c")
    plane = lax.axis_index(("x", "y"))
    planes = XS * YS
    layer = lax.axis_index(Z)
    layers = lax.axis_size(Z)
    odd_layer = lax.axis_index("zl")
    odd_x = lax.axis_index("x") % 2
    parity = (odd_x + odd_layer) % 2
    dp_index = plane * CS + core

    quarter = vocab_slab // 4

    def from_neighbour(part, axes, ahead):
        size = lax.axis_size(axes)
        pairs = [((k + ahead) % size, k) for k in range(size)]
        return lax.ppermute(embedding[part * quarter : (part + 1) * quarter], axes, pairs)

    pieces = (
        from_neighbour(0, Z, 1),
        from_neighbour(1, Z, -1),
        from_neighbour(2, "x", 1),
        from_neighbour(3, "x", -1),
    )
    along_x = lax.axis_index("x")
    slab_column = jnp.arange(vocab_slab, dtype=jnp.int32)
    near_layer = jnp.where(slab_column < quarter, layer + 1, layer)
    near_layer = jnp.where(slab_column // quarter == 1, layer - 1, near_layer) % layers
    near_x = jnp.where(slab_column // quarter == 2, along_x + 1, along_x)
    near_x = jnp.where(slab_column // quarter == 3, along_x - 1, near_x) % XS
    near_plane = near_x * YS + lax.axis_index("y")
    entry = jnp.concatenate(
        [
            ((at_plane * CS + which) * layers + at_layer) * vocab_slab + slab_column
            for at_plane, at_layer in ((plane, layer), (near_plane, near_layer))
            for which in (core, 1 - core)
        ]
    )

    held = jnp.concatenate([prompt_keys[0], prompt_values[0]], axis=1)
    arrived = spread(held, ("x", "y"))
    by_device = completion_prompt.reshape(planes * CS, comp_count)
    my_prompts = by_device[dp_index]
    partner_prompts = by_device[plane * CS + (1 - core)]
    mine = arrived[my_prompts // CS]
    for_partner = arrived[partner_prompts // CS]
    from_partner = lax.ppermute(for_partner, "c", SWAP)
    here = (my_prompts % CS) == core
    chosen = jnp.where(here[:, None, None], mine, from_partner)
    half = chosen.shape[2] // 2
    key_block = jnp.concatenate([chosen[:, :, :half], own_keys.reshape(comp_count, CLEN, -1)], axis=1)
    key_block = key_block.reshape(comp_count, prompt_span + CLEN, key_heads, HDIM)
    value_block = jnp.concatenate(
        [chosen[:, :, half:], own_values.reshape(comp_count, CLEN, -1)], axis=1
    )
    value_block = value_block.reshape(comp_count, prompt_span + CLEN, key_heads, HDIM)
    inside = jnp.arange(prompt_span)[None, :] < prompt_lengths[my_prompts][:, None]
    causal = jnp.arange(CLEN)[:, None] >= jnp.arange(CLEN)[None, :]
    visible = jnp.concatenate(
        [
            jnp.broadcast_to(inside[:, None, :], (comp_count, CLEN, prompt_span)),
            jnp.broadcast_to(causal[None], (comp_count, CLEN, CLEN)),
        ],
        axis=2,
    )
    attended = attend_local(
        queries.reshape(comp_count, CLEN, heads_here, HDIM), key_block, value_block, visible
    )
    partial_value = jnp.dot(attended, out_proj, preferred_element_type=jnp.float32)

    partial_value, pieces = lax.optimization_barrier((partial_value, pieces))

    share = row_count // layers
    head_total = summed(partial_value, Z)
    head_total, pieces, own = lax.optimization_barrier((head_total, pieces, embedding))
    near = join(pieces)
    slabs = (embedding, lax.ppermute(own, "c", SWAP), near, lax.ppermute(near, "c", SWAP))
    my_residual = lax.dynamic_slice_in_dim(residual, layer * share, share)
    hidden = my_residual.astype(jnp.float32) + head_total
    norm_factor = lax.rsqrt(jnp.mean(hidden * hidden, axis=-1, keepdims=True) + norm_epsilon)
    normed = (hidden * norm_factor * norm_gain).astype(jnp.bfloat16)

    pairs = layers // 2
    by_parity = spread(normed, Z).reshape(pairs, 2, share, width).transpose(1, 0, 2, 3)
    by_parity = by_parity.reshape(2, pairs * share, width)
    rows_here = planes * pairs * share
    for_even_x = jnp.where(odd_layer == 0, by_parity[0], by_parity[1])
    for_odd_x = jnp.where(odd_layer == 0, by_parity[1], by_parity[0])
    to_odd_x = (jnp.arange(planes) // YS % 2 == 1)[:, None, None]
    outgoing = jnp.where(to_odd_x, for_odd_x[None], for_even_x[None])
    every_row = lax.all_to_all(outgoing, ("x", "y"), 0, 0, tiled=True).reshape(rows_here, width)

    def of_rows(values):
        return values.reshape(planes, CS, pairs, 2, share)[:, core, :, parity].reshape(rows_here)

    def even_first(both, odd):
        return jnp.where(odd == 0, both, both[::-1])

    hit = entry[:, None] == of_rows(targets)[None, :]
    numbers = jnp.arange(entry.shape[0], dtype=jnp.int32)[:, None]
    target_column = jnp.max(jnp.where(hit, numbers, -1), axis=0, keepdims=True)
    logits, stats = slab_logits(every_row, target_column, slabs)
    every = spread(stats[:3], ("x", "y") + Z)
    every = every.reshape(XS // 2, 2, YS, pairs, 2, 3, rows_here)

    def of_parity(odd):
        picks = [every[:, at_x, :, :, (at_x + odd) % 2] for at_x in range(2)]
        return merged(jnp.stack(picks).reshape(-1, 3, rows_here))

    stats = jnp.stack([of_parity(0), of_parity(1)])
    log_total = stats[:, 0] + jnp.log(stats[:, 1])
    every_logprob = (stats[:, 2] - log_total).reshape(2, planes, pairs, share)
    logprob = every_logprob[:, plane].transpose(1, 0, 2).reshape(row_count)

    row_ids = jnp.arange(targets.shape[0], dtype=jnp.int32)
    live_token = row_ids % CLEN < jnp.repeat(completion_lengths, CLEN)
    token_weight = of_rows(jnp.where(live_token, -jnp.repeat(advantages, CLEN), 0.0))
    terms = slab_gradient(
        logits, target_column, log_total[parity][None], token_weight[None], slabs
    )
    arrived = lax.all_to_all(
        terms.reshape(planes, pairs * share, width), ("x", "y"), 0, 0, tiled=True
    )
    arrived = arrived.reshape(XS // 2, 2, YS, pairs * share, width).astype(jnp.float32)
    both = even_first(jnp.sum(arrived, axis=(0, 2)), odd_layer)
    both = both.reshape(2, pairs, share, width).transpose(1, 0, 2, 3).reshape(row_count, width)
    normed_grad = summed(both.astype(jnp.bfloat16), Z)
    hidden_grad = norm_gain * norm_factor * normed_grad - hidden * norm_factor**3 * jnp.mean(
        norm_gain * normed_grad * hidden, axis=-1, keepdims=True
    )
    hidden_grad = spread(hidden_grad.astype(jnp.bfloat16), Z).reshape(row_count, width)
    return (logprob, hidden_grad.astype(jnp.float32))


def solution(mesh):
    fine = Mesh(mesh.devices.reshape(XS, YS, CS, -1, 2), ("x", "y", "c") + Z)
    dp = ("x", "y", "c")
    placed = (
        P(dp, Z),
        P(dp, Z),
        P(dp, Z),
        P(dp, None, Z),
        P(dp, None, Z),
        P(),
        P(),
        P(),
        P(),
        P(),
        P(dp, None),
        P(Z, None),
        P(),
        P(dp + Z, None),
    )
    return jax.shard_map(
        body, mesh=fine, in_specs=placed, out_specs=(P(dp), P(dp, None)), check_vma=False
    )
```

```python
import jax
import jax.numpy as jnp
from jax import lax
from jax.experimental import pallas as pl
from jax.experimental.pallas import tpu as pltpu
from jax.sharding import Mesh
from jax.sharding import PartitionSpec as P

HDIM = 128
CLEN = 8
XS, YS, CS = 4, 4, 2

score_scale = 168.0 ** (-0.5)
norm_epsilon = 1e-06
SWAP = ((0, 1), (1, 0))
Z = ("zh", "zl")


def spread(part, axes):
    count = lax.axis_size(axes)
    copies = jnp.broadcast_to(part[None], (count,) + part.shape)
    return lax.all_to_all(copies, axes, 0, 0, tiled=True)


def summed(rows, axes):
    count = lax.axis_size(axes)
    pieces = rows.reshape(count, rows.shape[0] // count, rows.shape[1])
    arrived = lax.all_to_all(pieces, axes, 0, 0, tiled=True)
    return jnp.sum(arrived.astype(jnp.float32), axis=0)


def attend_local(queries, key_block, value_block, visible):
    comp_count, step_count, heads_here, head_width = queries.shape
    key_heads = key_block.shape[2]
    group_size = heads_here // key_heads
    grouped = queries.reshape(comp_count, step_count, key_heads, group_size, head_width)
    scores = (
        jnp.einsum("ctkgd,cnkd->ctkgn", grouped, key_block, preferred_element_type=jnp.float32)
        * score_scale
    )
    scores = jnp.where(visible[:, :, None, None, :], scores, -jnp.inf)
    row_top = jnp.max(scores, axis=-1, keepdims=True)
    exp_scores = jnp.exp(scores - row_top)
    weights = (exp_scores / jnp.sum(exp_scores, axis=-1, keepdims=True)).astype(jnp.bfloat16)
    mixed_values = jnp.einsum(
        "ctkgn,cnkd->ctkgd", weights, value_block, preferred_element_type=jnp.float32
    )
    return mixed_values.reshape(comp_count * step_count, heads_here * head_width).astype(
        jnp.bfloat16
    )


def merged(stats):
    top = jnp.max(stats[:, 0], axis=0)
    total = jnp.sum(stats[:, 1] * jnp.exp(stats[:, 0] - top[None]), axis=0)
    return jnp.stack([top, total, jnp.sum(stats[:, 2], axis=0)])


NT = (((1,), (1,)), ((), ()))


def placed_rows(parts):
    starts = [0]
    for part in parts:
        starts.append(starts[-1] + part.shape[0])
    return starts


def logits_kernel(rows, target_column, *refs):
    parts, (logits, stats, held, held_rows, arrivals, rows_arrival) = refs[:-6], refs[-6:]
    starts = placed_rows(parts)
    rows_copy = pltpu.make_async_copy(rows, held_rows, rows_arrival)
    rows_copy.start()
    copies = [
        pltpu.make_async_copy(part, held.at[pl.ds(start, part.shape[0])], arrivals.at[k])
        for k, (part, start) in enumerate(zip(parts, starts))
    ]
    for copy in copies:
        copy.start()
    rows_copy.wait()
    depth = parts[0].shape[0]
    top = total = picked = None
    for start in range(0, starts[-1], depth):
        for copy, at in zip(copies, starts):
            if start <= at < start + depth:
                copy.wait()
        block = lax.dot_general(
            held[pl.ds(start, depth), :], held_rows[...], NT, preferred_element_type=jnp.float32
        )
        logits[pl.ds(start, depth), :] = block
        hit = lax.broadcasted_iota(jnp.int32, block.shape, 0) + start == target_column[...]
        block_picked = jnp.sum(jnp.where(hit, block, 0.0), axis=0, keepdims=True)
        block_top = jnp.max(block, axis=0, keepdims=True)
        new_top = block_top if start == 0 else jnp.maximum(top, block_top)
        block_total = jnp.sum(jnp.exp(block - new_top), axis=0, keepdims=True)
        total = block_total if start == 0 else total * jnp.exp(top - new_top) + block_total
        picked = block_picked if start == 0 else picked + block_picked
        top = new_top
    line = lax.broadcasted_iota(jnp.int32, stats.shape, 0)
    stats[...] = jnp.where(line == 0, top, jnp.where(line == 1, total, picked))


def gradient_kernel(logits, target_column, log_total, token_weight, *refs):
    parts, (terms, held, held_logits, grad, arrivals, logits_arrival) = refs[:-6], refs[-6:]
    starts = placed_rows(parts)
    tile = held.shape[2]
    steps = terms.shape[1] // tile

    def fetch(step):
        slot = step % 2
        copies = [
            pltpu.make_async_copy(
                part.at[:, pl.ds(step * tile, tile)],
                held.at[slot, pl.ds(start, part.shape[0])],
                arrivals.at[slot, k],
            )
            for k, (part, start) in enumerate(zip(parts, starts))
        ]
        for copy in copies:
            copy.start()
        return copies

    logits_copy = pltpu.make_async_copy(logits, held_logits, logits_arrival)
    logits_copy.start()
    coming = fetch(0)
    logits_copy.wait()
    chunk = parts[0].shape[0] // 2
    for start in range(0, starts[-1], chunk):
        block = held_logits[pl.ds(start, chunk), :]
        hit = lax.broadcasted_iota(jnp.int32, block.shape, 0) + start == target_column[...]
        block = jnp.where(hit, 1.0, 0.0) - jnp.exp(block - log_total[...])
        grad[:, pl.ds(start, chunk)] = (token_weight[...] * block).T.astype(jnp.bfloat16)
    for step in range(steps):
        following = fetch(step + 1) if step + 1 < steps else None
        for copy in coming:
            copy.wait()
        coming = following
        terms[:, pl.ds(step * tile, tile)] = jnp.dot(
            grad[...], held[step % 2], preferred_element_type=jnp.float32
        ).astype(jnp.bfloat16)


def slab_logits(rows, target_column, parts):
    width = rows.shape[1]
    count, entries = rows.shape[0], placed_rows(parts)[-1]
    whole = pl.BlockSpec(memory_space=pltpu.VMEM)
    remain = pl.BlockSpec(memory_space=pltpu.HBM)
    return pl.pallas_call(
        logits_kernel,
        out_shape=(
            jax.ShapeDtypeStruct((entries, count), jnp.float32),
            jax.ShapeDtypeStruct((8, count), jnp.float32),
        ),
        in_specs=[remain, whole] + [remain] * len(parts),
        out_specs=[whole, whole],
        scratch_shapes=[
            pltpu.VMEM((entries, width), jnp.bfloat16),
            pltpu.VMEM((count, width), jnp.bfloat16),
            pltpu.SemaphoreType.DMA((len(parts),)),
            pltpu.SemaphoreType.DMA,
        ],
        compiler_params=pltpu.CompilerParams(vmem_limit_bytes=44 * 1024 * 1024),
        cost_estimate=pl.CostEstimate(
            flops=2 * count * entries * width,
            bytes_accessed=2 * entries * width,
            transcendentals=count * entries,
        ),
    )(rows, target_column, *parts)


def slab_gradient(logits, target_column, log_total, token_weight, parts):
    width = parts[0].shape[1]
    entries, count = logits.shape
    tile = next(t for t in (768, 512, 256, 128) if width % t == 0)
    whole = pl.BlockSpec(memory_space=pltpu.VMEM)
    remain = pl.BlockSpec(memory_space=pltpu.HBM)
    return pl.pallas_call(
        gradient_kernel,
        out_shape=jax.ShapeDtypeStruct((count, width), jnp.bfloat16),
        in_specs=[remain] + [whole] * 3 + [remain] * len(parts),
        out_specs=whole,
        scratch_shapes=[
            pltpu.VMEM((2, entries, tile), jnp.bfloat16),
            pltpu.VMEM((entries, count), jnp.float32),
            pltpu.VMEM((count, entries), jnp.bfloat16),
            pltpu.SemaphoreType.DMA((2, len(parts))),
            pltpu.SemaphoreType.DMA,
        ],
        compiler_params=pltpu.CompilerParams(vmem_limit_bytes=44 * 1024 * 1024),
        cost_estimate=pl.CostEstimate(
            flops=2 * count * entries * width,
            bytes_accessed=2 * entries * width,
            transcendentals=count * entries,
        ),
    )(logits, target_column, log_total, token_weight, *parts)


def body(
    queries,
    own_keys,
    own_values,
    prompt_keys,
    prompt_values,
    prompt_lengths,
    completion_prompt,
    completion_lengths,
    targets,
    advantages,
    residual,
    out_proj,
    norm_gain,
    embedding,
):
    row_count, width = residual.shape
    comp_count = row_count // CLEN
    heads_here = queries.shape[1] // HDIM
    key_heads = own_keys.shape[1] // HDIM
    prompt_span = prompt_keys.shape[1]
    vocab_slab = embedding.shape[0]
    core = lax.axis_index("c")
    plane = lax.axis_index(("x", "y"))
    planes = XS * YS
    layer = lax.axis_index(Z)
    layers = lax.axis_size(Z)
    along_x, along_y = lax.axis_index("x"), lax.axis_index("y")
    parity = (along_x + along_y) % 2
    dp_index = plane * CS + core

    quarter = vocab_slab // 4

    def from_neighbour(part, axes, ahead):
        size = lax.axis_size(axes)
        pairs = [((k + ahead) % size, k) for k in range(size)]
        return lax.ppermute(embedding[part * quarter : (part + 1) * quarter], axes, pairs)

    pieces = (
        from_neighbour(0, "x", 1),
        from_neighbour(1, "x", -1),
        from_neighbour(2, "y", 1),
        from_neighbour(3, "y", -1),
    )
    slab_column = jnp.arange(vocab_slab, dtype=jnp.int32)
    source = slab_column // quarter
    near_x = along_x + jnp.where(source == 0, 1, 0) - jnp.where(source == 1, 1, 0)
    near_y = along_y + jnp.where(source == 2, 1, 0) - jnp.where(source == 3, 1, 0)
    near_plane = near_x % XS * YS + near_y % YS
    entry = jnp.concatenate(
        [
            ((at_plane * CS + which) * layers + layer) * vocab_slab + slab_column
            for at_plane in (plane, near_plane)
            for which in (core, 1 - core)
        ]
    )

    held = jnp.concatenate([prompt_keys[0], prompt_values[0]], axis=1)
    arrived = spread(held, ("x", "y"))
    by_device = completion_prompt.reshape(planes * CS, comp_count)
    my_prompts = by_device[dp_index]
    partner_prompts = by_device[plane * CS + (1 - core)]
    mine = arrived[my_prompts // CS]
    for_partner = arrived[partner_prompts // CS]
    from_partner = lax.ppermute(for_partner, "c", SWAP)
    here = (my_prompts % CS) == core
    chosen = jnp.where(here[:, None, None], mine, from_partner)
    half = chosen.shape[2] // 2
    key_block = jnp.concatenate([chosen[:, :, :half], own_keys.reshape(comp_count, CLEN, -1)], axis=1)
    key_block = key_block.reshape(comp_count, prompt_span + CLEN, key_heads, HDIM)
    value_block = jnp.concatenate(
        [chosen[:, :, half:], own_values.reshape(comp_count, CLEN, -1)], axis=1
    )
    value_block = value_block.reshape(comp_count, prompt_span + CLEN, key_heads, HDIM)
    inside = jnp.arange(prompt_span)[None, :] < prompt_lengths[my_prompts][:, None]
    causal = jnp.arange(CLEN)[:, None] >= jnp.arange(CLEN)[None, :]
    visible = jnp.concatenate(
        [
            jnp.broadcast_to(inside[:, None, :], (comp_count, CLEN, prompt_span)),
            jnp.broadcast_to(causal[None], (comp_count, CLEN, CLEN)),
        ],
        axis=2,
    )
    attended = attend_local(
        queries.reshape(comp_count, CLEN, heads_here, HDIM), key_block, value_block, visible
    )
    partial_value = jnp.dot(attended, out_proj, preferred_element_type=jnp.float32)


    share = row_count // layers
    head_total = summed(partial_value, Z)
    my_residual = lax.dynamic_slice_in_dim(residual, layer * share, share)
    hidden = my_residual.astype(jnp.float32) + head_total
    norm_factor = lax.rsqrt(jnp.mean(hidden * hidden, axis=-1, keepdims=True) + norm_epsilon)
    normed = (hidden * norm_factor * norm_gain).astype(jnp.bfloat16)

    pairs = layers // 2
    by_parity = spread(normed, Z)
    by_parity, pieces, own = lax.optimization_barrier((by_parity, pieces, embedding))
    swapped = [lax.ppermute(part, "c", SWAP) for part in (own,) + tuple(pieces)]
    parts = (embedding, swapped[0]) + tuple(pieces) + tuple(swapped[1:])
    by_parity = by_parity.reshape(pairs, 2, share, width).transpose(1, 0, 2, 3)
    by_parity = by_parity.reshape(2, pairs * share, width)
    rows_here = planes * pairs * share
    to_plane = jnp.arange(planes)
    to_odd = ((to_plane // YS + to_plane) % 2 == 1)[:, None, None]
    outgoing = jnp.where(to_odd, by_parity[1][None], by_parity[0][None])
    every_row = lax.all_to_all(outgoing, ("x", "y"), 0, 0, tiled=True).reshape(rows_here, width)

    def of_rows(values):
        return values.reshape(planes, CS, pairs, 2, share)[:, core, :, parity].reshape(rows_here)

    hit = entry[:, None] == of_rows(targets)[None, :]
    numbers = jnp.arange(entry.shape[0], dtype=jnp.int32)[:, None]
    target_column = jnp.max(jnp.where(hit, numbers, -1), axis=0, keepdims=True)
    logits, stats = slab_logits(every_row, target_column, parts)
    stats = merged(spread(stats[:3], Z))
    stats = spread(stats, ("x", "y")).reshape(XS // 2, 2, YS // 2, 2, 3, rows_here)

    def of_parity(odd):
        picks = [stats[:, at_x, :, (at_x + odd) % 2] for at_x in range(2)]
        return merged(jnp.stack(picks).reshape(-1, 3, rows_here))

    stats = jnp.stack([of_parity(0), of_parity(1)])
    log_total = stats[:, 0] + jnp.log(stats[:, 1])
    every_logprob = (stats[:, 2] - log_total).reshape(2, planes, pairs, share)
    logprob = every_logprob[:, plane].transpose(1, 0, 2).reshape(row_count)

    row_ids = jnp.arange(targets.shape[0], dtype=jnp.int32)
    live_token = row_ids % CLEN < jnp.repeat(completion_lengths, CLEN)
    token_weight = of_rows(jnp.where(live_token, -jnp.repeat(advantages, CLEN), 0.0))
    terms = slab_gradient(
        logits, target_column, log_total[parity][None], token_weight[None], parts
    )
    arrived = lax.all_to_all(
        terms.reshape(planes, pairs * share, width), ("x", "y"), 0, 0, tiled=True
    )
    arrived = arrived.astype(jnp.float32)
    both = jnp.stack(
        [
            jnp.sum(jnp.where(to_odd, 0.0, arrived), axis=0),
            jnp.sum(jnp.where(to_odd, arrived, 0.0), axis=0),
        ]
    )
    both = both.reshape(2, pairs, share, width).transpose(1, 0, 2, 3).reshape(row_count, width)
    normed_grad = summed(both.astype(jnp.bfloat16), Z)
    hidden_grad = norm_gain * norm_factor * normed_grad - hidden * norm_factor**3 * jnp.mean(
        norm_gain * normed_grad * hidden, axis=-1, keepdims=True
    )
    hidden_grad = spread(hidden_grad.astype(jnp.bfloat16), Z).reshape(row_count, width)
    return (logprob, hidden_grad.astype(jnp.float32))


def solution(mesh):
    fine = Mesh(mesh.devices.reshape(XS, YS, CS, -1, 2), ("x", "y", "c") + Z)
    dp = ("x", "y", "c")
    placed = (
        P(dp, Z),
        P(dp, Z),
        P(dp, Z),
        P(dp, None, Z),
        P(dp, None, Z),
        P(),
        P(),
        P(),
        P(),
        P(),
        P(dp, None),
        P(Z, None),
        P(),
        P(dp + Z, None),
    )
    return jax.shard_map(
        body, mesh=fine, in_specs=placed, out_specs=(P(dp), P(dp, None)), check_vma=False
    )
```

```python
import jax
import jax.numpy as jnp
from jax import lax
from jax.experimental import pallas as pl
from jax.experimental.pallas import tpu as pltpu
from jax.sharding import Mesh
from jax.sharding import PartitionSpec as P

HDIM = 128
CLEN = 8
XS, YS, CS = 4, 4, 2

score_scale = 168.0 ** (-0.5)
norm_epsilon = 1e-06
SWAP = ((0, 1), (1, 0))
Z = ("zh", "zl")


def spread(part, axes):
    count = lax.axis_size(axes)
    copies = jnp.broadcast_to(part[None], (count,) + part.shape)
    return lax.all_to_all(copies, axes, 0, 0, tiled=True)


def summed(rows, axes):
    count = lax.axis_size(axes)
    pieces = rows.reshape(count, rows.shape[0] // count, rows.shape[1])
    arrived = lax.all_to_all(pieces, axes, 0, 0, tiled=True)
    return jnp.sum(arrived.astype(jnp.float32), axis=0)


def attend_local(queries, key_block, value_block, visible):
    comp_count, step_count, heads_here, head_width = queries.shape
    key_heads = key_block.shape[2]
    group_size = heads_here // key_heads
    grouped = queries.reshape(comp_count, step_count, key_heads, group_size, head_width)
    scores = (
        jnp.einsum("ctkgd,cnkd->ctkgn", grouped, key_block, preferred_element_type=jnp.float32)
        * score_scale
    )
    scores = jnp.where(visible[:, :, None, None, :], scores, -jnp.inf)
    row_top = jnp.max(scores, axis=-1, keepdims=True)
    exp_scores = jnp.exp(scores - row_top)
    weights = (exp_scores / jnp.sum(exp_scores, axis=-1, keepdims=True)).astype(jnp.bfloat16)
    mixed_values = jnp.einsum(
        "ctkgn,cnkd->ctkgd", weights, value_block, preferred_element_type=jnp.float32
    )
    return mixed_values.reshape(comp_count * step_count, heads_here * head_width).astype(
        jnp.bfloat16
    )


def merged(stats):
    top = jnp.max(stats[:, 0], axis=0)
    total = jnp.sum(stats[:, 1] * jnp.exp(stats[:, 0] - top[None]), axis=0)
    return jnp.stack([top, total, jnp.sum(stats[:, 2], axis=0)])


NT = (((1,), (1,)), ((), ()))


def placed_rows(parts):
    starts = [0]
    for part in parts:
        starts.append(starts[-1] + part.shape[0])
    return starts


def logits_kernel(rows, target_column, own, across, *refs):
    pieces, (logits, stats, near, held_rows, arrivals, rows_arrival) = refs[:-6], refs[-6:]
    rows_copy = pltpu.make_async_copy(rows, held_rows, rows_arrival)
    rows_copy.start()
    copies = [
        pltpu.make_async_copy(piece, near.at[pl.ds(start, piece.shape[0])], arrivals.at[k])
        for k, (piece, start) in enumerate(zip(pieces, placed_rows(pieces)))
    ]
    for copy in copies:
        copy.start()
    rows_copy.wait()
    depth = own.shape[0]
    half = len(pieces) // 2
    top = total = picked = None
    for k in range(4):
        start = k * depth
        for copy in copies[(k - 2) * half : (k - 1) * half] if k >= 2 else ():
            copy.wait()
        slab = (own, across)[k] if k < 2 else near.at[pl.ds((k - 2) * depth, depth)]
        block = lax.dot_general(
            held_rows[...], slab[...], NT, preferred_element_type=jnp.float32
        )
        logits[:, pl.ds(start, depth)] = block
        hit = lax.broadcasted_iota(jnp.int32, block.shape, 1) + start == target_column[...]
        block_picked = jnp.sum(jnp.where(hit, block, 0.0), axis=1, keepdims=True)
        block_top = jnp.max(block, axis=1, keepdims=True)
        new_top = block_top if k == 0 else jnp.maximum(top, block_top)
        block_total = jnp.sum(jnp.exp(block - new_top), axis=1, keepdims=True)
        total = block_total if k == 0 else total * jnp.exp(top - new_top) + block_total
        picked = block_picked if k == 0 else picked + block_picked
        top = new_top
    lane = lax.broadcasted_iota(jnp.int32, stats.shape, 1)
    stats[...] = jnp.where(lane == 0, top, jnp.where(lane == 1, total, picked))


def gradient_kernel(logits, target_column, log_total, token_weight, own, across, *refs):
    pieces, (terms, near, held_logits, grad, arrivals, logits_arrival) = refs[:-6], refs[-6:]
    starts = placed_rows(pieces)
    tile = near.shape[2]
    steps = terms.shape[1] // tile
    depth = own.shape[0]

    def fetch(step):
        slot = step % 2
        copies = [
            pltpu.make_async_copy(
                piece.at[:, pl.ds(step * tile, tile)],
                near.at[slot, pl.ds(start, piece.shape[0])],
                arrivals.at[slot, k],
            )
            for k, (piece, start) in enumerate(zip(pieces, starts))
        ]
        for copy in copies:
            copy.start()
        return copies

    logits_copy = pltpu.make_async_copy(logits, held_logits, logits_arrival)
    logits_copy.start()
    coming = fetch(0)
    logits_copy.wait()
    for start in range(0, 4 * depth, depth):
        block = held_logits[:, pl.ds(start, depth)]
        hit = lax.broadcasted_iota(jnp.int32, block.shape, 1) + start == target_column[...]
        block = jnp.where(hit, 1.0, 0.0) - jnp.exp(block - log_total[...])
        grad[:, pl.ds(start, depth)] = (token_weight[...] * block).astype(jnp.bfloat16)
    for step in range(steps):
        following = fetch(step + 1) if step + 1 < steps else None
        here = pl.ds(step * tile, tile)
        mixed = jnp.dot(
            grad[:, pl.ds(0, depth)], own[:, here], preferred_element_type=jnp.float32
        ) + jnp.dot(
            grad[:, pl.ds(depth, depth)], across[:, here], preferred_element_type=jnp.float32
        )
        for copy in coming:
            copy.wait()
        coming = following
        mixed += jnp.dot(
            grad[:, pl.ds(2 * depth, 2 * depth)],
            near[step % 2],
            preferred_element_type=jnp.float32,
        )
        terms[:, here] = mixed.astype(jnp.bfloat16)


WHOLE = pl.BlockSpec(memory_space=pltpu.VMEM)
REMAIN = pl.BlockSpec(memory_space=pltpu.HBM)
LIMIT = pltpu.CompilerParams(vmem_limit_bytes=26 * 1024 * 1024)


def slab_cost(count, entries, width):
    return pl.CostEstimate(
        flops=2 * count * entries * width,
        bytes_accessed=2 * entries * width,
        transcendentals=count * entries,
    )


def slab_logits(rows, target_column, slabs, pieces):
    (count, width), depth = rows.shape, slabs[0].shape[0]
    return pl.pallas_call(
        logits_kernel,
        out_shape=(
            jax.ShapeDtypeStruct((count, 4 * depth), jnp.float32),
            jax.ShapeDtypeStruct((count, 128), jnp.float32),
        ),
        in_specs=[REMAIN] + [WHOLE] * 3 + [REMAIN] * len(pieces),
        out_specs=[WHOLE, WHOLE],
        scratch_shapes=[
            pltpu.VMEM((2 * depth, width), jnp.bfloat16),
            pltpu.VMEM((count, width), jnp.bfloat16),
            pltpu.SemaphoreType.DMA((len(pieces),)),
            pltpu.SemaphoreType.DMA,
        ],
        compiler_params=LIMIT,
        cost_estimate=slab_cost(count, 4 * depth, width),
    )(rows, target_column, *slabs, *pieces)


def slab_gradient(logits, target_column, log_total, token_weight, slabs, pieces):
    (depth, width), count = slabs[0].shape, logits.shape[0]
    tile = next(t for t in (1792, 512, 256, 128) if width % t == 0)
    return pl.pallas_call(
        gradient_kernel,
        out_shape=jax.ShapeDtypeStruct((count, width), jnp.bfloat16),
        in_specs=[REMAIN] + [WHOLE] * 5 + [REMAIN] * len(pieces),
        out_specs=WHOLE,
        scratch_shapes=[
            pltpu.VMEM((2, 2 * depth, tile), jnp.bfloat16),
            pltpu.VMEM((count, 4 * depth), jnp.float32),
            pltpu.VMEM((count, 4 * depth), jnp.bfloat16),
            pltpu.SemaphoreType.DMA((2, len(pieces))),
            pltpu.SemaphoreType.DMA,
        ],
        compiler_params=LIMIT,
        cost_estimate=slab_cost(count, 4 * depth, width),
    )(logits, target_column, log_total, token_weight, *slabs, *pieces)


def body(
    queries,
    own_keys,
    own_values,
    prompt_keys,
    prompt_values,
    prompt_lengths,
    completion_prompt,
    completion_lengths,
    targets,
    advantages,
    residual,
    out_proj,
    norm_gain,
    embedding,
):
    row_count, width = residual.shape
    comp_count = row_count // CLEN
    heads_here = queries.shape[1] // HDIM
    key_heads = own_keys.shape[1] // HDIM
    prompt_span = prompt_keys.shape[1]
    vocab_slab = embedding.shape[0]
    core = lax.axis_index("c")
    plane = lax.axis_index(("x", "y"))
    planes = XS * YS
    layer = lax.axis_index(Z)
    layers = lax.axis_size(Z)
    along_x, along_y = lax.axis_index("x"), lax.axis_index("y")
    parity = (along_x + along_y) % 2
    dp_index = plane * CS + core

    quarter = vocab_slab // 4

    def from_neighbour(part, axes, ahead):
        size = lax.axis_size(axes)
        pairs = [((k + ahead) % size, k) for k in range(size)]
        return lax.ppermute(embedding[part * quarter : (part + 1) * quarter], axes, pairs)

    pieces = (
        from_neighbour(0, "x", 1),
        from_neighbour(1, "x", -1),
        from_neighbour(2, "y", 1),
        from_neighbour(3, "y", -1),
    )
    slab_column = jnp.arange(vocab_slab, dtype=jnp.int32)
    source = slab_column // quarter
    near_x = along_x + jnp.where(source == 0, 1, 0) - jnp.where(source == 1, 1, 0)
    near_y = along_y + jnp.where(source == 2, 1, 0) - jnp.where(source == 3, 1, 0)
    near_plane = near_x % XS * YS + near_y % YS
    entry = jnp.concatenate(
        [
            ((at_plane * CS + which) * layers + layer) * vocab_slab + slab_column
            for at_plane in (plane, near_plane)
            for which in (core, 1 - core)
        ]
    )

    held = jnp.concatenate([prompt_keys[0], prompt_values[0]], axis=1)
    arrived = spread(held, ("x", "y"))
    by_device = completion_prompt.reshape(planes * CS, comp_count)
    my_prompts = by_device[dp_index]
    partner_prompts = by_device[plane * CS + (1 - core)]
    mine = arrived[my_prompts // CS]
    for_partner = arrived[partner_prompts // CS]
    from_partner = lax.ppermute(for_partner, "c", SWAP)
    here = (my_prompts % CS) == core
    chosen = jnp.where(here[:, None, None], mine, from_partner)
    half = chosen.shape[2] // 2
    key_block = jnp.concatenate([chosen[:, :, :half], own_keys.reshape(comp_count, CLEN, -1)], axis=1)
    key_block = key_block.reshape(comp_count, prompt_span + CLEN, key_heads, HDIM)
    value_block = jnp.concatenate(
        [chosen[:, :, half:], own_values.reshape(comp_count, CLEN, -1)], axis=1
    )
    value_block = value_block.reshape(comp_count, prompt_span + CLEN, key_heads, HDIM)
    inside = jnp.arange(prompt_span)[None, :] < prompt_lengths[my_prompts][:, None]
    causal = jnp.arange(CLEN)[:, None] >= jnp.arange(CLEN)[None, :]
    visible = jnp.concatenate(
        [
            jnp.broadcast_to(inside[:, None, :], (comp_count, CLEN, prompt_span)),
            jnp.broadcast_to(causal[None], (comp_count, CLEN, CLEN)),
        ],
        axis=2,
    )
    attended = attend_local(
        queries.reshape(comp_count, CLEN, heads_here, HDIM), key_block, value_block, visible
    )
    partial_value = jnp.dot(attended, out_proj, preferred_element_type=jnp.float32)


    share = row_count // layers
    head_total = summed(partial_value, Z)
    my_residual = lax.dynamic_slice_in_dim(residual, layer * share, share)
    hidden = my_residual.astype(jnp.float32) + head_total
    norm_factor = lax.rsqrt(jnp.mean(hidden * hidden, axis=-1, keepdims=True) + norm_epsilon)
    normed = (hidden * norm_factor * norm_gain).astype(jnp.bfloat16)

    pairs = layers // 2
    by_parity = spread(normed, Z)
    by_parity, pieces, own = lax.optimization_barrier((by_parity, pieces, embedding))
    swapped = [lax.ppermute(part, "c", SWAP) for part in (own,) + tuple(pieces)]
    slabs, near = (embedding, swapped[0]), tuple(pieces) + tuple(swapped[1:])
    by_parity = by_parity.reshape(pairs, 2, share, width).transpose(1, 0, 2, 3)
    by_parity = by_parity.reshape(2, pairs * share, width)
    rows_here = planes * pairs * share
    to_plane = jnp.arange(planes)
    to_odd = ((to_plane // YS + to_plane) % 2 == 1)[:, None, None]
    outgoing = jnp.where(to_odd, by_parity[1][None], by_parity[0][None])
    every_row = lax.all_to_all(outgoing, ("x", "y"), 0, 0, tiled=True).reshape(rows_here, width)

    def of_rows(values):
        return values.reshape(planes, CS, pairs, 2, share)[:, core, :, parity].reshape(rows_here)

    hit = entry[None, :] == of_rows(targets)[:, None]
    numbers = jnp.arange(entry.shape[0], dtype=jnp.int32)[None, :]
    target_column = jnp.max(jnp.where(hit, numbers, -1), axis=1, keepdims=True)
    logits, stats = slab_logits(every_row, target_column, slabs, near)
    stats = merged(spread(stats[:, :3].T, Z))
    stats = spread(stats, ("x", "y")).reshape(XS // 2, 2, YS // 2, 2, 3, rows_here)

    def of_parity(odd):
        picks = [stats[:, at_x, :, (at_x + odd) % 2] for at_x in range(2)]
        return merged(jnp.stack(picks).reshape(-1, 3, rows_here))

    stats = jnp.stack([of_parity(0), of_parity(1)])
    log_total = stats[:, 0] + jnp.log(stats[:, 1])
    every_logprob = (stats[:, 2] - log_total).reshape(2, planes, pairs, share)
    logprob = every_logprob[:, plane].transpose(1, 0, 2).reshape(row_count)

    row_ids = jnp.arange(targets.shape[0], dtype=jnp.int32)
    live_token = row_ids % CLEN < jnp.repeat(completion_lengths, CLEN)
    token_weight = of_rows(jnp.where(live_token, -jnp.repeat(advantages, CLEN), 0.0))
    terms = slab_gradient(
        logits, target_column, log_total[parity][:, None], token_weight[:, None], slabs, near
    )
    arrived = lax.all_to_all(
        terms.reshape(planes, pairs * share, width), ("x", "y"), 0, 0, tiled=True
    )
    arrived = arrived.astype(jnp.float32)
    both = jnp.stack(
        [
            jnp.sum(jnp.where(to_odd, 0.0, arrived), axis=0),
            jnp.sum(jnp.where(to_odd, arrived, 0.0), axis=0),
        ]
    )
    both = both.reshape(2, pairs, share, width).transpose(1, 0, 2, 3).reshape(row_count, width)
    normed_grad = summed(both.astype(jnp.bfloat16), Z)
    hidden_grad = norm_gain * norm_factor * normed_grad - hidden * norm_factor**3 * jnp.mean(
        norm_gain * normed_grad * hidden, axis=-1, keepdims=True
    )
    hidden_grad = spread(hidden_grad.astype(jnp.bfloat16), Z).reshape(row_count, width)
    return (logprob, hidden_grad.astype(jnp.float32))


def solution(mesh):
    fine = Mesh(mesh.devices.reshape(XS, YS, CS, -1, 2), ("x", "y", "c") + Z)
    dp = ("x", "y", "c")
    placed = (
        P(dp, Z),
        P(dp, Z),
        P(dp, Z),
        P(dp, None, Z),
        P(dp, None, Z),
        P(),
        P(),
        P(),
        P(),
        P(),
        P(dp, None),
        P(Z, None),
        P(),
        P(dp + Z, None),
    )
    return jax.shard_map(
        body, mesh=fine, in_specs=placed, out_specs=(P(dp), P(dp, None)), check_vma=False
    )
```

```python
import jax
import jax.numpy as jnp
from jax import lax
from jax.experimental import pallas as pl
from jax.experimental.pallas import tpu as pltpu
from jax.sharding import Mesh
from jax.sharding import PartitionSpec as P

HDIM = 128
CLEN = 8
XS, YS, CS = 4, 4, 2

score_scale = 168.0 ** (-0.5)
norm_epsilon = 1e-06
SWAP = ((0, 1), (1, 0))
Z = ("zh", "zl")


def spread(part, axes):
    count = lax.axis_size(axes)
    copies = jnp.broadcast_to(part[None], (count,) + part.shape)
    return lax.all_to_all(copies, axes, 0, 0, tiled=True)


def summed(rows, axes):
    count = lax.axis_size(axes)
    pieces = rows.reshape(count, rows.shape[0] // count, rows.shape[1])
    arrived = lax.all_to_all(pieces, axes, 0, 0, tiled=True)
    return jnp.sum(arrived.astype(jnp.float32), axis=0)


def attend_local(queries, key_block, value_block, visible):
    comp_count, step_count, heads_here, head_width = queries.shape
    key_heads = key_block.shape[2]
    group_size = heads_here // key_heads
    grouped = queries.reshape(comp_count, step_count, key_heads, group_size, head_width)
    scores = (
        jnp.einsum("ctkgd,cnkd->ctkgn", grouped, key_block, preferred_element_type=jnp.float32)
        * score_scale
    )
    scores = jnp.where(visible[:, :, None, None, :], scores, -jnp.inf)
    row_top = jnp.max(scores, axis=-1, keepdims=True)
    exp_scores = jnp.exp(scores - row_top)
    weights = (exp_scores / jnp.sum(exp_scores, axis=-1, keepdims=True)).astype(jnp.bfloat16)
    mixed_values = jnp.einsum(
        "ctkgn,cnkd->ctkgd", weights, value_block, preferred_element_type=jnp.float32
    )
    return mixed_values.reshape(comp_count * step_count, heads_here * head_width).astype(
        jnp.bfloat16
    )


def merged(stats):
    top = jnp.max(stats[:, 0], axis=0)
    total = jnp.sum(stats[:, 1] * jnp.exp(stats[:, 0] - top[None]), axis=0)
    return jnp.stack([top, total, jnp.sum(stats[:, 2], axis=0)])


NT = (((1,), (1,)), ((), ()))


def placed_rows(parts):
    starts = [0]
    for part in parts:
        starts.append(starts[-1] + part.shape[0])
    return starts


def logits_kernel(rows, target_column, *refs):
    parts, (logits, stats, held, held_rows, arrivals, rows_arrival) = refs[:-6], refs[-6:]
    starts = placed_rows(parts)
    rows_copy = pltpu.make_async_copy(rows, held_rows, rows_arrival)
    rows_copy.start()
    copies = [
        pltpu.make_async_copy(part, held.at[pl.ds(start, part.shape[0])], arrivals.at[k])
        for k, (part, start) in enumerate(zip(parts, starts))
    ]
    for copy in copies:
        copy.start()
    rows_copy.wait()
    depth = parts[0].shape[0]
    top = total = picked = None
    for start in range(0, starts[-1], depth):
        for copy, at in zip(copies, starts):
            if start <= at < start + depth:
                copy.wait()
        block = lax.dot_general(
            held_rows[...], held[pl.ds(start, depth), :], NT, preferred_element_type=jnp.float32
        )
        logits[:, pl.ds(start, depth)] = block
        hit = lax.broadcasted_iota(jnp.int32, block.shape, 1) + start == target_column[...]
        block_picked = jnp.sum(jnp.where(hit, block, 0.0), axis=1, keepdims=True)
        block_top = jnp.max(block, axis=1, keepdims=True)
        new_top = block_top if start == 0 else jnp.maximum(top, block_top)
        block_total = jnp.sum(jnp.exp(block - new_top), axis=1, keepdims=True)
        total = block_total if start == 0 else total * jnp.exp(top - new_top) + block_total
        picked = block_picked if start == 0 else picked + block_picked
        top = new_top
    lane = lax.broadcasted_iota(jnp.int32, stats.shape, 1)
    stats[...] = jnp.where(lane == 0, top, jnp.where(lane == 1, total, picked))


def gradient_kernel(logits, target_column, log_total, token_weight, *refs):
    parts, (terms, held, held_logits, grad, arrivals, logits_arrival) = refs[:-6], refs[-6:]
    starts = placed_rows(parts)
    tile = held.shape[2]
    steps = terms.shape[1] // tile

    def fetch(step):
        slot = step % 2
        copies = [
            pltpu.make_async_copy(
                part.at[:, pl.ds(step * tile, tile)],
                held.at[slot, pl.ds(start, part.shape[0])],
                arrivals.at[slot, k],
            )
            for k, (part, start) in enumerate(zip(parts, starts))
        ]
        for copy in copies:
            copy.start()
        return copies

    logits_copy = pltpu.make_async_copy(logits, held_logits, logits_arrival)
    logits_copy.start()
    coming = fetch(0)
    logits_copy.wait()
    depth = parts[0].shape[0]
    for start in range(0, starts[-1], depth):
        block = held_logits[:, pl.ds(start, depth)]
        hit = lax.broadcasted_iota(jnp.int32, block.shape, 1) + start == target_column[...]
        block = jnp.where(hit, 1.0, 0.0) - jnp.exp(block - log_total[...])
        grad[:, pl.ds(start, depth)] = (token_weight[...] * block).astype(jnp.bfloat16)
    for step in range(steps):
        following = fetch(step + 1) if step + 1 < steps else None
        for copy in coming:
            copy.wait()
        coming = following
        terms[:, pl.ds(step * tile, tile)] = jnp.dot(
            grad[...], held[step % 2], preferred_element_type=jnp.float32
        ).astype(jnp.bfloat16)


def slab_logits(rows, target_column, parts):
    width = rows.shape[1]
    count, entries = rows.shape[0], placed_rows(parts)[-1]
    whole = pl.BlockSpec(memory_space=pltpu.VMEM)
    remain = pl.BlockSpec(memory_space=pltpu.HBM)
    return pl.pallas_call(
        logits_kernel,
        out_shape=(
            jax.ShapeDtypeStruct((count, entries), jnp.float32),
            jax.ShapeDtypeStruct((count, 128), jnp.float32),
        ),
        in_specs=[remain, whole] + [remain] * len(parts),
        out_specs=[whole, whole],
        scratch_shapes=[
            pltpu.VMEM((entries, width), jnp.bfloat16),
            pltpu.VMEM((count, width), jnp.bfloat16),
            pltpu.SemaphoreType.DMA((len(parts),)),
            pltpu.SemaphoreType.DMA,
        ],
        compiler_params=pltpu.CompilerParams(vmem_limit_bytes=48 * 1024 * 1024),
        cost_estimate=pl.CostEstimate(
            flops=2 * count * entries * width,
            bytes_accessed=2 * entries * width,
            transcendentals=count * entries,
        ),
    )(rows, target_column, *parts)


def slab_gradient(logits, target_column, log_total, token_weight, parts):
    width = parts[0].shape[1]
    count, entries = logits.shape
    tile = next(t for t in (1792, 512, 256, 128) if width % t == 0)
    whole = pl.BlockSpec(memory_space=pltpu.VMEM)
    remain = pl.BlockSpec(memory_space=pltpu.HBM)
    return pl.pallas_call(
        gradient_kernel,
        out_shape=jax.ShapeDtypeStruct((count, width), jnp.bfloat16),
        in_specs=[remain] + [whole] * 3 + [remain] * len(parts),
        out_specs=whole,
        scratch_shapes=[
            pltpu.VMEM((2, entries, tile), jnp.bfloat16),
            pltpu.VMEM((count, entries), jnp.float32),
            pltpu.VMEM((count, entries), jnp.bfloat16),
            pltpu.SemaphoreType.DMA((2, len(parts))),
            pltpu.SemaphoreType.DMA,
        ],
        compiler_params=pltpu.CompilerParams(vmem_limit_bytes=48 * 1024 * 1024),
        cost_estimate=pl.CostEstimate(
            flops=2 * count * entries * width,
            bytes_accessed=2 * entries * width,
            transcendentals=count * entries,
        ),
    )(logits, target_column, log_total, token_weight, *parts)


def body(
    queries,
    own_keys,
    own_values,
    prompt_keys,
    prompt_values,
    prompt_lengths,
    completion_prompt,
    completion_lengths,
    targets,
    advantages,
    residual,
    out_proj,
    norm_gain,
    embedding,
):
    held = jnp.concatenate([prompt_keys[0], prompt_values[0]], axis=1)
    arrived, rest = lax.optimization_barrier(
        (
            spread(held, ("x", "y")),
            (
                queries,
                own_keys,
                own_values,
                prompt_lengths,
                completion_prompt,
                completion_lengths,
                targets,
                advantages,
                residual,
                embedding,
            ),
        )
    )
    queries, own_keys, own_values, prompt_lengths, completion_prompt = rest[:5]
    completion_lengths, targets, advantages, residual, embedding = rest[5:]
    row_count, width = residual.shape
    comp_count = row_count // CLEN
    heads_here = queries.shape[1] // HDIM
    key_heads = own_keys.shape[1] // HDIM
    prompt_span = prompt_keys.shape[1]
    vocab_slab = embedding.shape[0]
    core = lax.axis_index("c")
    plane = lax.axis_index(("x", "y"))
    planes = XS * YS
    layer = lax.axis_index(Z)
    layers = lax.axis_size(Z)
    along_x, along_y = lax.axis_index("x"), lax.axis_index("y")
    parity = (along_x + along_y) % 2
    dp_index = plane * CS + core

    quarter = vocab_slab // 4

    def from_neighbour(part, axes, ahead):
        size = lax.axis_size(axes)
        pairs = [((k + ahead) % size, k) for k in range(size)]
        return lax.ppermute(embedding[part * quarter : (part + 1) * quarter], axes, pairs)

    pieces = (
        from_neighbour(0, "x", 1),
        from_neighbour(1, "x", -1),
        from_neighbour(2, "y", 1),
        from_neighbour(3, "y", -1),
    )
    slab_column = jnp.arange(vocab_slab, dtype=jnp.int32)
    source = slab_column // quarter
    near_x = along_x + jnp.where(source == 0, 1, 0) - jnp.where(source == 1, 1, 0)
    near_y = along_y + jnp.where(source == 2, 1, 0) - jnp.where(source == 3, 1, 0)
    near_plane = near_x % XS * YS + near_y % YS
    entry = jnp.concatenate(
        [
            ((at_plane * CS + which) * layers + layer) * vocab_slab + slab_column
            for at_plane in (plane, near_plane)
            for which in (core, 1 - core)
        ]
    )

    by_device = completion_prompt.reshape(planes * CS, comp_count)
    my_prompts = by_device[dp_index]
    partner_prompts = by_device[plane * CS + (1 - core)]
    mine = arrived[my_prompts // CS]
    for_partner = arrived[partner_prompts // CS]
    from_partner = lax.ppermute(for_partner, "c", SWAP)
    here = (my_prompts % CS) == core
    chosen = jnp.where(here[:, None, None], mine, from_partner)
    half = chosen.shape[2] // 2
    key_block = jnp.concatenate([chosen[:, :, :half], own_keys.reshape(comp_count, CLEN, -1)], axis=1)
    key_block = key_block.reshape(comp_count, prompt_span + CLEN, key_heads, HDIM)
    value_block = jnp.concatenate(
        [chosen[:, :, half:], own_values.reshape(comp_count, CLEN, -1)], axis=1
    )
    value_block = value_block.reshape(comp_count, prompt_span + CLEN, key_heads, HDIM)
    inside = jnp.arange(prompt_span)[None, :] < prompt_lengths[my_prompts][:, None]
    causal = jnp.arange(CLEN)[:, None] >= jnp.arange(CLEN)[None, :]
    visible = jnp.concatenate(
        [
            jnp.broadcast_to(inside[:, None, :], (comp_count, CLEN, prompt_span)),
            jnp.broadcast_to(causal[None], (comp_count, CLEN, CLEN)),
        ],
        axis=2,
    )
    attended = attend_local(
        queries.reshape(comp_count, CLEN, heads_here, HDIM), key_block, value_block, visible
    )
    partial_value = jnp.dot(attended, out_proj, preferred_element_type=jnp.float32)


    share = row_count // layers
    head_total = summed(partial_value, Z)
    my_residual = lax.dynamic_slice_in_dim(residual, layer * share, share)
    hidden = my_residual.astype(jnp.float32) + head_total
    norm_factor = lax.rsqrt(jnp.mean(hidden * hidden, axis=-1, keepdims=True) + norm_epsilon)
    normed = (hidden * norm_factor * norm_gain).astype(jnp.bfloat16)

    pairs = layers // 2
    by_parity = spread(normed, Z)
    by_parity, pieces, own = lax.optimization_barrier((by_parity, pieces, embedding))
    swapped = [lax.ppermute(part, "c", SWAP) for part in (own,) + tuple(pieces)]
    parts = (embedding, swapped[0]) + tuple(pieces) + tuple(swapped[1:])
    by_parity = by_parity.reshape(pairs, 2, share, width).transpose(1, 0, 2, 3)
    by_parity = by_parity.reshape(2, pairs * share, width)
    rows_here = planes * pairs * share
    to_plane = jnp.arange(planes)
    to_odd = ((to_plane // YS + to_plane) % 2 == 1)[:, None, None]
    outgoing = jnp.where(to_odd, by_parity[1][None], by_parity[0][None])
    every_row = lax.all_to_all(outgoing, ("x", "y"), 0, 0, tiled=True).reshape(rows_here, width)

    def of_rows(values):
        return values.reshape(planes, CS, pairs, 2, share)[:, core, :, parity].reshape(rows_here)

    hit = entry[None, :] == of_rows(targets)[:, None]
    numbers = jnp.arange(entry.shape[0], dtype=jnp.int32)[None, :]
    target_column = jnp.max(jnp.where(hit, numbers, -1), axis=1, keepdims=True)
    row_ids = jnp.arange(targets.shape[0], dtype=jnp.int32)
    live_token = row_ids % CLEN < jnp.repeat(completion_lengths, CLEN)
    token_weight = of_rows(jnp.where(live_token, -jnp.repeat(advantages, CLEN), 0.0))[:, None]
    logits, stats = slab_logits(every_row, target_column, parts)

    stats, later = lax.optimization_barrier(
        (stats[:, :3].T, (logits, target_column, token_weight, hidden, norm_factor, norm_gain))
    )
    stats, later = lax.optimization_barrier((spread(stats, Z), later))
    stats, later = lax.optimization_barrier((merged(stats), later))
    stats, later = lax.optimization_barrier((spread(stats, ("x", "y")), later))
    logits, target_column, token_weight, hidden, norm_factor, norm_gain = later
    stats = stats.reshape(XS // 2, 2, YS // 2, 2, 3, rows_here)

    def of_parity(odd):
        picks = [stats[:, at_x, :, (at_x + odd) % 2] for at_x in range(2)]
        return merged(jnp.stack(picks).reshape(-1, 3, rows_here))

    stats = jnp.stack([of_parity(0), of_parity(1)])
    log_total = stats[:, 0] + jnp.log(stats[:, 1])
    every_logprob = (stats[:, 2] - log_total).reshape(2, planes, pairs, share)
    logprob = every_logprob[:, plane].transpose(1, 0, 2).reshape(row_count)

    terms = slab_gradient(
        logits, target_column, log_total[parity][:, None], token_weight, parts
    )
    arrived = lax.all_to_all(
        terms.reshape(planes, pairs * share, width), ("x", "y"), 0, 0, tiled=True
    )
    arrived = arrived.astype(jnp.float32)
    both = jnp.stack(
        [
            jnp.sum(jnp.where(to_odd, 0.0, arrived), axis=0),
            jnp.sum(jnp.where(to_odd, arrived, 0.0), axis=0),
        ]
    )
    both = both.reshape(2, pairs, share, width).transpose(1, 0, 2, 3).reshape(row_count, width)
    normed_grad = summed(both.astype(jnp.bfloat16), Z)
    hidden_grad = norm_gain * norm_factor * normed_grad - hidden * norm_factor**3 * jnp.mean(
        norm_gain * normed_grad * hidden, axis=-1, keepdims=True
    )
    hidden_grad, logprob = lax.optimization_barrier((hidden_grad.astype(jnp.bfloat16), logprob))
    hidden_grad = spread(hidden_grad, Z).reshape(row_count, width)
    return (logprob, hidden_grad.astype(jnp.float32))


def solution(mesh):
    fine = Mesh(mesh.devices.reshape(XS, YS, CS, -1, 2), ("x", "y", "c") + Z)
    dp = ("x", "y", "c")
    placed = (
        P(dp, Z),
        P(dp, Z),
        P(dp, Z),
        P(dp, None, Z),
        P(dp, None, Z),
        P(),
        P(),
        P(),
        P(),
        P(),
        P(dp, None),
        P(Z, None),
        P(),
        P(dp + Z, None),
    )
    return jax.shard_map(
        body, mesh=fine, in_specs=placed, out_specs=(P(dp), P(dp, None)), check_vma=False
    )
```

```python
import jax
import jax.numpy as jnp
from jax import lax
from jax.experimental import pallas as pl
from jax.experimental.pallas import tpu as pltpu
from jax.sharding import Mesh
from jax.sharding import PartitionSpec as P

HDIM = 128
CLEN = 8
XS, YS, CS = 4, 4, 2

score_scale = 168.0 ** (-0.5)
norm_epsilon = 1e-06
SWAP = ((0, 1), (1, 0))
Z = ("zh", "zl")


def spread(part, axes):
    count = lax.axis_size(axes)
    copies = jnp.broadcast_to(part[None], (count,) + part.shape)
    return lax.all_to_all(copies, axes, 0, 0, tiled=True)


def summed(rows, axes):
    count = lax.axis_size(axes)
    pieces = rows.reshape(count, rows.shape[0] // count, rows.shape[1])
    arrived = lax.all_to_all(pieces, axes, 0, 0, tiled=True)
    return jnp.sum(arrived.astype(jnp.float32), axis=0)


def attend_local(queries, key_block, value_block, visible):
    comp_count, step_count, heads_here, head_width = queries.shape
    key_heads = key_block.shape[2]
    group_size = heads_here // key_heads
    grouped = queries.reshape(comp_count, step_count, key_heads, group_size, head_width)
    scores = (
        jnp.einsum("ctkgd,cnkd->ctkgn", grouped, key_block, preferred_element_type=jnp.float32)
        * score_scale
    )
    scores = jnp.where(visible[:, :, None, None, :], scores, -jnp.inf)
    row_top = jnp.max(scores, axis=-1, keepdims=True)
    exp_scores = jnp.exp(scores - row_top)
    weights = (exp_scores / jnp.sum(exp_scores, axis=-1, keepdims=True)).astype(jnp.bfloat16)
    mixed_values = jnp.einsum(
        "ctkgn,cnkd->ctkgd", weights, value_block, preferred_element_type=jnp.float32
    )
    return mixed_values.reshape(comp_count * step_count, heads_here * head_width).astype(
        jnp.bfloat16
    )


def spread_stats(stats, axes):
    filled = jnp.concatenate([stats.reshape(-1), jnp.zeros_like(stats[0])])
    arrived = spread(filled.reshape(-1, 128), axes)
    return arrived.reshape(arrived.shape[0], 4, -1)[:, :3]


def merged(stats):
    top = jnp.max(stats[:, 0], axis=0)
    total = jnp.sum(stats[:, 1] * jnp.exp(stats[:, 0] - top[None]), axis=0)
    return jnp.stack([top, total, jnp.sum(stats[:, 2], axis=0)])


NT = (((1,), (1,)), ((), ()))


def placed_rows(parts):
    starts = [0]
    for part in parts:
        starts.append(starts[-1] + part.shape[0])
    return starts


def logits_kernel(rows, target_column, *refs):
    parts, (logits, stats, held, arrivals) = refs[:-4], refs[-4:]
    starts = placed_rows(parts)
    copies = [
        pltpu.make_async_copy(part, held.at[pl.ds(start, part.shape[0])], arrivals.at[k])
        for k, (part, start) in enumerate(zip(parts, starts))
    ]
    for copy in copies:
        copy.start()
    depth = parts[0].shape[0]
    top = total = picked = None
    for start in range(0, starts[-1], depth):
        for copy, at in zip(copies, starts):
            if start <= at < start + depth:
                copy.wait()
        block = lax.dot_general(
            rows[...], held[pl.ds(start, depth), :], NT, preferred_element_type=jnp.float32
        )
        logits[:, pl.ds(start, depth)] = block
        hit = lax.broadcasted_iota(jnp.int32, block.shape, 1) + start == target_column[...]
        block_picked = jnp.sum(jnp.where(hit, block, 0.0), axis=1, keepdims=True)
        block_top = jnp.max(block, axis=1, keepdims=True)
        new_top = block_top if start == 0 else jnp.maximum(top, block_top)
        block_total = jnp.sum(jnp.exp(block - new_top), axis=1, keepdims=True)
        total = block_total if start == 0 else total * jnp.exp(top - new_top) + block_total
        picked = block_picked if start == 0 else picked + block_picked
        top = new_top
    lane = lax.broadcasted_iota(jnp.int32, stats.shape, 1)
    stats[...] = jnp.where(lane == 0, top, jnp.where(lane == 1, total, picked))


def gradient_kernel(logits, target_column, log_total, token_weight, *refs):
    parts, (terms, held, held_logits, grad, arrivals, logits_arrival) = refs[:-6], refs[-6:]
    starts = placed_rows(parts)
    tile = held.shape[2]
    steps = terms.shape[1] // tile

    def fetch(step):
        slot = step % 2
        copies = [
            pltpu.make_async_copy(
                part.at[:, pl.ds(step * tile, tile)],
                held.at[slot, pl.ds(start, part.shape[0])],
                arrivals.at[slot, k],
            )
            for k, (part, start) in enumerate(zip(parts, starts))
        ]
        for copy in copies:
            copy.start()
        return copies

    logits_copy = pltpu.make_async_copy(logits, held_logits, logits_arrival)
    logits_copy.start()
    coming = fetch(0)
    logits_copy.wait()
    depth = parts[0].shape[0]
    for start in range(0, starts[-1], depth):
        block = held_logits[:, pl.ds(start, depth)]
        hit = lax.broadcasted_iota(jnp.int32, block.shape, 1) + start == target_column[...]
        block = jnp.where(hit, 1.0, 0.0) - jnp.exp(block - log_total[...])
        grad[:, pl.ds(start, depth)] = (token_weight[...] * block).astype(jnp.bfloat16)
    for step in range(steps):
        following = fetch(step + 1) if step + 1 < steps else None
        for copy in coming:
            copy.wait()
        coming = following
        terms[:, pl.ds(step * tile, tile)] = jnp.dot(
            grad[...], held[step % 2], preferred_element_type=jnp.float32
        ).astype(jnp.bfloat16)


def slab_logits(rows, target_column, parts):
    width = rows.shape[1]
    count, entries = rows.shape[0], placed_rows(parts)[-1]
    whole = pl.BlockSpec(memory_space=pltpu.VMEM)
    remain = pl.BlockSpec(memory_space=pltpu.HBM)
    return pl.pallas_call(
        logits_kernel,
        out_shape=(
            jax.ShapeDtypeStruct((count, entries), jnp.float32),
            jax.ShapeDtypeStruct((count, 128), jnp.float32),
        ),
        in_specs=[whole, whole] + [remain] * len(parts),
        out_specs=[whole, whole],
        scratch_shapes=[
            pltpu.VMEM((entries, width), jnp.bfloat16),
            pltpu.SemaphoreType.DMA((len(parts),)),
        ],
        compiler_params=pltpu.CompilerParams(vmem_limit_bytes=32 * 1024 * 1024),
        cost_estimate=pl.CostEstimate(
            flops=2 * count * entries * width,
            bytes_accessed=2 * entries * width,
            transcendentals=count * entries,
        ),
    )(rows, target_column, *parts)


def slab_gradient(logits, target_column, log_total, token_weight, parts):
    width = parts[0].shape[1]
    count, entries = logits.shape
    tile = next(t for t in (1792, 512, 256, 128) if width % t == 0)
    whole = pl.BlockSpec(memory_space=pltpu.VMEM)
    remain = pl.BlockSpec(memory_space=pltpu.HBM)
    return pl.pallas_call(
        gradient_kernel,
        out_shape=jax.ShapeDtypeStruct((count, width), jnp.bfloat16),
        in_specs=[remain] + [whole] * 3 + [remain] * len(parts),
        out_specs=whole,
        scratch_shapes=[
            pltpu.VMEM((2, entries, tile), jnp.bfloat16),
            pltpu.VMEM((count, entries), jnp.float32),
            pltpu.VMEM((count, entries), jnp.bfloat16),
            pltpu.SemaphoreType.DMA((2, len(parts))),
            pltpu.SemaphoreType.DMA,
        ],
        compiler_params=pltpu.CompilerParams(vmem_limit_bytes=48 * 1024 * 1024),
        cost_estimate=pl.CostEstimate(
            flops=2 * count * entries * width,
            bytes_accessed=2 * entries * width,
            transcendentals=count * entries,
        ),
    )(logits, target_column, log_total, token_weight, *parts)


def body(
    queries,
    own_keys,
    own_values,
    prompt_keys,
    prompt_values,
    prompt_lengths,
    completion_prompt,
    completion_lengths,
    targets,
    advantages,
    residual,
    out_proj,
    norm_gain,
    embedding,
):
    held = jnp.concatenate([prompt_keys[0], prompt_values[0]], axis=1)
    arrived, rest = lax.optimization_barrier(
        (
            spread(held, ("x", "y")),
            (
                queries,
                own_keys,
                own_values,
                prompt_lengths,
                completion_prompt,
                completion_lengths,
                targets,
                advantages,
                residual,
                embedding,
            ),
        )
    )
    queries, own_keys, own_values, prompt_lengths, completion_prompt = rest[:5]
    completion_lengths, targets, advantages, residual, embedding = rest[5:]
    row_count, width = residual.shape
    comp_count = row_count // CLEN
    heads_here = queries.shape[1] // HDIM
    key_heads = own_keys.shape[1] // HDIM
    prompt_span = prompt_keys.shape[1]
    vocab_slab = embedding.shape[0]
    core = lax.axis_index("c")
    plane = lax.axis_index(("x", "y"))
    planes = XS * YS
    layer = lax.axis_index(Z)
    layers = lax.axis_size(Z)
    along_x, along_y = lax.axis_index("x"), lax.axis_index("y")
    parity = (along_x + along_y) % 2
    dp_index = plane * CS + core

    quarter = vocab_slab // 4

    def from_neighbour(part, axes, ahead):
        size = lax.axis_size(axes)
        pairs = [((k + ahead) % size, k) for k in range(size)]
        return lax.ppermute(embedding[part * quarter : (part + 1) * quarter], axes, pairs)

    pieces = (
        from_neighbour(0, "x", 1),
        from_neighbour(1, "x", -1),
        from_neighbour(2, "y", 1),
        from_neighbour(3, "y", -1),
    )
    slab_column = jnp.arange(vocab_slab, dtype=jnp.int32)
    source = slab_column // quarter
    near_x = along_x + jnp.where(source == 0, 1, 0) - jnp.where(source == 1, 1, 0)
    near_y = along_y + jnp.where(source == 2, 1, 0) - jnp.where(source == 3, 1, 0)
    near_plane = near_x % XS * YS + near_y % YS
    entry = jnp.concatenate(
        [
            ((at_plane * CS + which) * layers + layer) * vocab_slab + slab_column
            for at_plane in (plane, near_plane)
            for which in (core, 1 - core)
        ]
    )

    by_device = completion_prompt.reshape(planes * CS, comp_count)
    my_prompts = by_device[dp_index]
    partner_prompts = by_device[plane * CS + (1 - core)]
    mine = arrived[my_prompts // CS]
    for_partner = arrived[partner_prompts // CS]
    from_partner = lax.ppermute(for_partner, "c", SWAP)
    here = (my_prompts % CS) == core
    chosen = jnp.where(here[:, None, None], mine, from_partner)
    half = chosen.shape[2] // 2
    key_block = jnp.concatenate([chosen[:, :, :half], own_keys.reshape(comp_count, CLEN, -1)], axis=1)
    key_block = key_block.reshape(comp_count, prompt_span + CLEN, key_heads, HDIM)
    value_block = jnp.concatenate(
        [chosen[:, :, half:], own_values.reshape(comp_count, CLEN, -1)], axis=1
    )
    value_block = value_block.reshape(comp_count, prompt_span + CLEN, key_heads, HDIM)
    inside = jnp.arange(prompt_span)[None, :] < prompt_lengths[my_prompts][:, None]
    causal = jnp.arange(CLEN)[:, None] >= jnp.arange(CLEN)[None, :]
    visible = jnp.concatenate(
        [
            jnp.broadcast_to(inside[:, None, :], (comp_count, CLEN, prompt_span)),
            jnp.broadcast_to(causal[None], (comp_count, CLEN, CLEN)),
        ],
        axis=2,
    )
    attended = attend_local(
        queries.reshape(comp_count, CLEN, heads_here, HDIM), key_block, value_block, visible
    )
    partial_value = jnp.dot(attended, out_proj, preferred_element_type=jnp.float32)


    share = row_count // layers
    head_total = summed(partial_value, Z)
    my_residual = lax.dynamic_slice_in_dim(residual, layer * share, share)
    hidden = my_residual.astype(jnp.float32) + head_total
    norm_factor = lax.rsqrt(jnp.mean(hidden * hidden, axis=-1, keepdims=True) + norm_epsilon)
    normed = (hidden * norm_factor * norm_gain).astype(jnp.bfloat16)

    pairs = layers // 2
    by_parity = spread(normed, Z)
    by_parity, pieces, own = lax.optimization_barrier((by_parity, pieces, embedding))
    swapped = [lax.ppermute(part, "c", SWAP) for part in (own,) + tuple(pieces)]
    parts = (embedding, swapped[0]) + tuple(pieces) + tuple(swapped[1:])
    by_parity = by_parity.reshape(pairs, 2, share, width).transpose(1, 0, 2, 3)
    by_parity = by_parity.reshape(2, pairs * share, width)
    rows_here = planes * pairs * share
    to_plane = jnp.arange(planes)
    to_odd = ((to_plane // YS + to_plane) % 2 == 1)[:, None, None]
    outgoing = jnp.where(to_odd, by_parity[1][None], by_parity[0][None])
    every_row = lax.all_to_all(outgoing, ("x", "y"), 0, 0, tiled=True).reshape(rows_here, width)

    def of_rows(values):
        return values.reshape(planes, CS, pairs, 2, share)[:, core, :, parity].reshape(rows_here)

    hit = entry[None, :] == of_rows(targets)[:, None]
    numbers = jnp.arange(entry.shape[0], dtype=jnp.int32)[None, :]
    target_column = jnp.max(jnp.where(hit, numbers, -1), axis=1, keepdims=True)
    row_ids = jnp.arange(targets.shape[0], dtype=jnp.int32)
    live_token = row_ids % CLEN < jnp.repeat(completion_lengths, CLEN)
    token_weight = of_rows(jnp.where(live_token, -jnp.repeat(advantages, CLEN), 0.0))[:, None]
    logits, stats = slab_logits(every_row, target_column, parts)

    stats, later = lax.optimization_barrier(
        (stats[:, :3].T, (logits, target_column, token_weight, hidden, norm_factor, norm_gain))
    )
    stats, later = lax.optimization_barrier((spread_stats(stats, Z), later))
    stats, later = lax.optimization_barrier((merged(stats), later))
    stats, later = lax.optimization_barrier((spread_stats(stats, ("x", "y")), later))
    logits, target_column, token_weight, hidden, norm_factor, norm_gain = later
    stats = stats.reshape(XS // 2, 2, YS // 2, 2, 3, rows_here)

    def of_parity(odd):
        picks = [stats[:, at_x, :, (at_x + odd) % 2] for at_x in range(2)]
        return merged(jnp.stack(picks).reshape(-1, 3, rows_here))

    stats = jnp.stack([of_parity(0), of_parity(1)])
    log_total = stats[:, 0] + jnp.log(stats[:, 1])
    every_logprob = (stats[:, 2] - log_total).reshape(2, planes, pairs, share)
    logprob = every_logprob[:, plane].transpose(1, 0, 2).reshape(row_count)

    terms = slab_gradient(
        logits, target_column, log_total[parity][:, None], token_weight, parts
    )
    arrived = lax.all_to_all(
        terms.reshape(planes, pairs * share, width), ("x", "y"), 0, 0, tiled=True
    )
    arrived = arrived.astype(jnp.float32)
    both = jnp.stack(
        [
            jnp.sum(jnp.where(to_odd, 0.0, arrived), axis=0),
            jnp.sum(jnp.where(to_odd, arrived, 0.0), axis=0),
        ]
    )
    both = both.reshape(2, pairs, share, width).transpose(1, 0, 2, 3).reshape(row_count, width)
    normed_grad = summed(both.astype(jnp.bfloat16), Z)
    hidden_grad = norm_gain * norm_factor * normed_grad - hidden * norm_factor**3 * jnp.mean(
        norm_gain * normed_grad * hidden, axis=-1, keepdims=True
    )
    hidden_grad, logprob = lax.optimization_barrier((hidden_grad.astype(jnp.bfloat16), logprob))
    hidden_grad = spread(hidden_grad, Z).reshape(row_count, width)
    return (logprob, hidden_grad.astype(jnp.float32))


def solution(mesh):
    fine = Mesh(mesh.devices.reshape(XS, YS, CS, -1, 2), ("x", "y", "c") + Z)
    dp = ("x", "y", "c")
    placed = (
        P(dp, Z),
        P(dp, Z),
        P(dp, Z),
        P(dp, None, Z),
        P(dp, None, Z),
        P(),
        P(),
        P(),
        P(),
        P(),
        P(dp, None),
        P(Z, None),
        P(),
        P(dp + Z, None),
    )
    return jax.shard_map(
        body, mesh=fine, in_specs=placed, out_specs=(P(dp), P(dp, None)), check_vma=False
    )
```
